32 devices in a mesh: gx: 8 (over z, y), gz: 4 (over x, core).
Axes of the slice: x: 2, y: 2, z: 4, core: 2. Of those that a mesh axis runs over, the one named last changes fastest.
Arguments:
- charge: float32 [32, 1024, 1024], P('gz', 'gx'), may hold values from -24 to 24
- cell_permittivity: float32 [32], replicated, may hold values from 1 to 4
- face_permittivity: float32 [32], replicated, may hold values from 1 to 4
- screening: float32 [32], replicated, may hold values from 0.001 to 0.01
Outputs:
- potential: float32 [32, 1024, 1024], P('gz', 'gx')
The draws below stay inside these ranges and needn't reach their ends.
All inputs are finite; a program needn't handle non-finite values.
Results may differ from the reference program's by a relative error of at most 0.0003.
Values sent between devices are 32-bit elements; how exact they have to be, the bound alone decides.
A program may use at most 128 MiB of HBM per device.

```python
import math
import jax
import jax.numpy as jnp
from jax import lax

NX = 1024
NY = 1024
NZ = 32


def block_scale(rng, shape, cuts, smallest, top_value):
    def one(dim, parts):
        steps = jax.random.uniform(jax.random.fold_in(jax.random.fold_in(rng, 6), dim), (parts,), jnp.float32, smallest / len(cuts), top_value / len(cuts))
        return jnp.repeat(jnp.exp(steps), shape[dim] // parts).reshape((-1,) + (1,) * (len(shape) - dim - 1))

    loudness = one(*cuts[0])
    for cut in cuts[1:]:
        loudness = loudness * one(*cut)
    return loudness


def normal_values(stream_key, shape, deviation, reach, split=(), held_as=jnp.bfloat16):
    array = jax.random.normal(stream_key, shape, jnp.float32) * deviation
    if len(split) > 0:
        array = block_scale(stream_key, shape, split, -0.22, 0.18) * array
    return jnp.clip(array, min=-reach, max=reach).astype(held_as)


def setup_inputs(seed: int = 0) -> dict:
    streams_of = jax.random.split(jax.random.key(seed), 5)
    return {
        "charge": normal_values(streams_of[0], (NZ, NX, NY), 4.0, 24.0, ((0, 4), (1, 8)), jnp.float32),
        "cell_permittivity": jnp.clip(jnp.exp(jax.random.uniform(streams_of[1], (NZ,), jnp.float32, math.log(1.0), math.log(4.0))), 1.0, 4.0),
        "face_permittivity": jnp.clip(jnp.exp(jax.random.uniform(streams_of[2], (NZ,), jnp.float32, math.log(1.0), math.log(4.0))), 1.0, 4.0),
        "screening": jnp.clip(jnp.exp(jax.random.uniform(streams_of[3], (NZ,), jnp.float32, math.log(0.001), math.log(0.01))), 0.001, 0.01),
    }


def mode_shift(count, length):
    frequency = jnp.arange(count, dtype=jnp.int32)
    angles = frequency.astype(jnp.float32) * (2.0 * math.pi / length)
    return 2.0 - 2.0 * jnp.cos(angles)


def reference(charge, cell_permittivity, face_permittivity, screening):
    layers = charge.shape[0]
    spectrum = jnp.fft.rfft2(charge, axes=(1, 2))
    half_width = NY // 2 + 1
    shifts = mode_shift(NX, NX)[:, None] + mode_shift(half_width, NY)[None, :]
    stacked = jnp.stack([jnp.real(spectrum), jnp.imag(spectrum)], axis=1).astype(jnp.float32)
    face_below = jnp.roll(face_permittivity, 1)
    layer_index = jnp.arange(layers, dtype=jnp.int32)
    sub_coef = jnp.where(layer_index > 0, -face_below, 0.0)
    sup_coef = jnp.where(layer_index < layers - 1, -face_permittivity, 0.0)

    def forward(carry, item):
        ratio_prev, part_prev = carry
        sub_one, sup_one, low_one, up_one, cell_one, scr_one, plane = item
        pivot = low_one + up_one + cell_one * shifts + scr_one - sub_one * ratio_prev
        ratio_next = sup_one / pivot
        part_next = (plane - sub_one * part_prev) / pivot[None]
        return (ratio_next, part_next), (ratio_next, part_next)

    start_carry = (jnp.zeros(shifts.shape, jnp.float32), jnp.zeros(stacked.shape[1:], jnp.float32))
    _, (ratios, partial_values) = lax.scan(forward, start_carry, (sub_coef, sup_coef, face_below, face_permittivity, cell_permittivity, screening, stacked))

    def backward(later, item):
        ratio_one, part_one = item
        value = part_one - ratio_one[None] * later
        return value, value

    _, solved = lax.scan(backward, jnp.zeros(stacked.shape[1:], jnp.float32), (ratios, partial_values), reverse=True)
    complex_field = lax.complex(solved[:, 0], solved[:, 1])
    potential = jnp.fft.irfft2(complex_field, s=(NX, NY), axes=(1, 2))
    return potential.astype(jnp.float32)
```

```python
import functools

import jax
import jax.numpy as jnp
import ml_dtypes
import numpy as np
from jax import lax
from jax.experimental import pallas as pl
from jax.experimental.pallas import tpu as pltpu
from jax.sharding import PartitionSpec as P

f32 = jnp.float32
bf16 = jnp.bfloat16
LANES = 256


def params(*semantics):
    return pltpu.CompilerParams(
        vmem_limit_bytes=48 * 1024 * 1024, dimension_semantics=semantics or ("arbitrary",)
    )


def cost(flops, moved):
    return pl.CostEstimate(flops=flops, bytes_accessed=moved, transcendentals=0)


def frequencies(length):
    col = np.arange(length)
    middle = length // 2
    return np.where(col <= middle, col, col - middle)


def basis_table(length):
    freq = frequencies(length)
    phase = (np.arange(length)[:, None] * freq[None, :]) % length
    angles = phase * (2.0 * np.pi / length)
    cos_part = np.arange(length)[None, :] <= length // 2
    return np.where(cos_part, np.cos(angles), np.sin(angles))


def halves(table):
    high = table.astype(ml_dtypes.bfloat16)
    low = (table - high.astype(np.float64)).astype(ml_dtypes.bfloat16)
    return high, low


def mode_weights(length):
    col = np.arange(length)
    edge = (col == 0) | (col == length // 2)
    return np.where(edge, 1.0 / length, 2.0 / length).astype(np.float32)


def mode_shift(length):
    return (2.0 - 2.0 * np.cos(frequencies(length) * (2.0 * np.pi / length))).astype(np.float32)


def split(value):
    high = value.astype(bf16)
    low = (value - high.astype(f32)).astype(bf16)
    return high, low


def product(left, right):
    dot = functools.partial(jnp.dot, preferred_element_type=f32)
    return dot(left[0], right[0]) + (dot(left[0], right[1]) + dot(left[1], right[0]))


def forward_y_kernel(charge_ref, high_ref, low_ref, out_ref, rows_high, rows_low):
    depth, x_local, width = charge_ref.shape
    m = out_ref.shape[2] // depth

    @pl.when(pl.program_id(0) == 0)
    def _():
        high, low = split(charge_ref[...].reshape(depth * x_local, width))
        rows_high[...] = high
        rows_low[...] = low

    result = product((rows_high[...], rows_low[...]), (high_ref[...], low_ref[...]))
    for group in range(out_ref.shape[0]):
        for z in range(depth):
            out_ref[group, :, z * m : (z + 1) * m] = result[
                z * x_local : (z + 1) * x_local, group * m : (group + 1) * m
            ]


def forward_y(charge, chunk, depth, high, low, groups):
    _, x_local, width = charge.shape
    m = width // groups
    per_step = min(groups, max(1, LANES // m))
    return pl.pallas_call(
        forward_y_kernel,
        out_shape=jax.ShapeDtypeStruct((groups, x_local, depth * m), f32),
        grid=(groups // per_step,),
        in_specs=[
            pl.BlockSpec((depth, x_local, width), lambda i: (chunk, 0, 0)),
            pl.BlockSpec((width, per_step * m), lambda i: (0, i)),
            pl.BlockSpec((width, per_step * m), lambda i: (0, i)),
        ],
        out_specs=pl.BlockSpec((per_step, x_local, depth * m), lambda i: (i, 0, 0)),
        scratch_shapes=[pltpu.VMEM((depth * x_local, width), bf16)] * 2,
        compiler_params=params(),
        cost_estimate=cost(6 * depth * x_local * width * width, 4 * width * width),
        name="forward_y",
    )(charge, high, low)


def left_multiply_kernel(value_ref, high_ref, low_ref, out_ref, part_high, part_low):
    @pl.when(pl.program_id(0) == 0)
    def _():
        high, low = split(value_ref[...])
        part_high[...] = high
        part_low[...] = low

    out_ref[...] = product((high_ref[...], low_ref[...]), (part_high[...], part_low[...]))


def left_multiply(high, low, value, name):
    length, columns = value.shape
    rows = min(256, length)
    return pl.pallas_call(
        left_multiply_kernel,
        out_shape=jax.ShapeDtypeStruct((length, columns), f32),
        grid=(length // rows,),
        in_specs=[
            pl.BlockSpec((length, columns), lambda i: (0, 0)),
            pl.BlockSpec((rows, length), lambda i: (i, 0)),
            pl.BlockSpec((rows, length), lambda i: (i, 0)),
        ],
        out_specs=pl.BlockSpec((rows, columns), lambda i: (i, 0)),
        scratch_shapes=[pltpu.VMEM((length, columns), bf16)] * 2,
        compiler_params=params(),
        cost_estimate=cost(6 * length * length * columns, 4 * length * length),
        name=name,
    )(value, high, low)


def back_y_kernel(value_ref, high_ref, low_ref, *rest):
    out_ref, rows_high, rows_low = rest[-3:]
    groups, x_local, columns = value_ref.shape
    depth = out_ref.shape[0]
    m = columns // depth

    @pl.when(pl.program_id(0) == 0)
    def _():
        for group in range(groups):
            high, low = split(value_ref[group])
            for z in range(depth):
                place = (slice(z * x_local, (z + 1) * x_local), slice(group * m, (group + 1) * m))
                rows_high[place] = high[:, z * m : (z + 1) * m]
                rows_low[place] = low[:, z * m : (z + 1) * m]

    result = product((rows_high[...], rows_low[...]), (high_ref[...], low_ref[...]))
    out_ref[...] = result.reshape(out_ref.shape)


def back_y(value, chunk, depth, slab_depth, high, low, held):
    groups, x_local, _ = value.shape
    width = high.shape[0]
    columns = min(LANES, width)
    operands = [value, high, low]
    in_specs = [
        pl.BlockSpec(value.shape, lambda i: (0, 0, 0)),
        pl.BlockSpec((width, columns), lambda i: (0, i)),
        pl.BlockSpec((width, columns), lambda i: (0, i)),
    ]
    aliases = {}
    if held is not None:
        operands.append(held)
        in_specs.append(pl.BlockSpec(memory_space=pl.ANY))
        aliases = {3: 0}
    return pl.pallas_call(
        back_y_kernel,
        out_shape=jax.ShapeDtypeStruct((slab_depth, x_local, width), f32),
        grid=(width // columns,),
        in_specs=in_specs,
        out_specs=pl.BlockSpec((depth, x_local, columns), lambda i: (chunk, 0, i)),
        scratch_shapes=[pltpu.VMEM((depth * x_local, width), bf16)] * 2,
        input_output_aliases=aliases,
        compiler_params=params(),
        cost_estimate=cost(6 * depth * x_local * width * width, 4 * width * width),
        name="back_y",
    )(*operands)


def pivots_kernel(
    layers, slab_depth, slab_ref, cell_ref, face_ref, screen_ref, shift_x, shift_y, inverse_ref, carry_ref
):
    shift = shift_x[...] + shift_y[...]
    slab = slab_ref[0]
    inverse = None
    for layer in range(layers):
        low = face_ref[(layer - 1) % layers]
        top = face_ref[layer]
        pivot = (low + top + screen_ref[layer]) + cell_ref[layer] * shift
        if layer > 0:
            pivot = pivot - (low * low) * inverse
        inverse = 1.0 / pivot
        place = layer % slab_depth
        group = layer // slab_depth

        @pl.when(slab == group)
        def _(place=place, inverse=inverse):
            inverse_ref[place] = inverse

        up, down = low * inverse, top * inverse
        if place == 0:
            rise, fall, both = up, down, up
        else:
            rise = rise * up
            both = both + rise * fall
            fall = fall * down
        if place == slab_depth - 1:
            carry_ref[group, 0] = rise
            carry_ref[group, 1] = both
            carry_ref[group, 2] = fall


def smem():
    return pl.BlockSpec(memory_space=pltpu.SMEM)


def pivots(slab, cell, face, screening, shift_x, shift_y, slab_depth):
    layers = cell.shape[0]
    length, m = shift_x.shape[0], shift_y.shape[1]
    slabs = layers // slab_depth
    rows = min(64, length)
    return pl.pallas_call(
        functools.partial(pivots_kernel, layers, slab_depth),
        out_shape=(
            jax.ShapeDtypeStruct((slab_depth, length, m), f32),
            jax.ShapeDtypeStruct((slabs, 3, length, m), f32),
        ),
        grid=(length // rows,),
        in_specs=[smem(), smem(), smem(), smem()]
        + [
            pl.BlockSpec((rows, 1), lambda i: (i, 0)),
            pl.BlockSpec((1, m), lambda i: (0, 0)),
        ],
        out_specs=(
            pl.BlockSpec((slab_depth, rows, m), lambda i: (0, i, 0)),
            pl.BlockSpec((slabs, 3, rows, m), lambda i: (0, 0, i, 0)),
        ),
        compiler_params=params(),
        cost_estimate=cost(20 * layers * length * m, 4 * length * m * (slab_depth + 3 * slabs)),
        name="pivots",
    )(slab, cell, face, screening, shift_x, shift_y)


def slab_faces(slab_ref, face_ref, slab_depth):
    layers = face_ref.shape[0]
    start = slab_ref[0] * slab_depth
    below = face_ref[lax.rem(start + (layers - 1), layers)]
    return [below] + [face_ref[start + place] for place in range(slab_depth)]


def sweep(planes, inverse_ref, faces, entering, leaving, m, depth):
    slab_depth = inverse_ref.shape[0]
    held = []
    value = entering
    for place in range(slab_depth):
        at = place % depth
        right = planes[place // depth][:, at * m : (at + 1) * m]
        if value is not None:
            right = right + faces[place] * value
        value = inverse_ref[place] * right
        held.append(value)
    last = value
    value = leaving
    for place in reversed(range(slab_depth)):
        if value is not None:
            held[place] = held[place] + (faces[place + 1] * inverse_ref[place]) * value
        value = held[place]
    return held, last


def ends_kernel(chunks, slab_ref, face_ref, inverse_ref, *rest):
    planes, out_ref = rest[:chunks], rest[-1]
    slab_depth, _, m = inverse_ref.shape
    faces = slab_faces(slab_ref, face_ref, slab_depth)
    solved, last = sweep(planes, inverse_ref, faces, None, None, m, slab_depth // chunks)
    out_ref[0] = last
    out_ref[1] = solved[0]


def ends(slab, face, inverse, planes):
    slab_depth, length, m = inverse.shape
    chunks = len(planes)
    rows = min(128, length)
    return pl.pallas_call(
        functools.partial(ends_kernel, chunks),
        out_shape=jax.ShapeDtypeStruct((2, length, m), f32),
        grid=(length // rows,),
        in_specs=[smem(), smem(), pl.BlockSpec((slab_depth, rows, m), lambda i: (0, i, 0))]
        + [pl.BlockSpec((rows, plane.shape[1]), lambda i: (i, 0)) for plane in planes],
        out_specs=pl.BlockSpec((2, rows, m), lambda i: (0, i, 0)),
        compiler_params=params(),
        cost_estimate=cost(6 * slab_depth * length * m, 8 * slab_depth * length * m),
        name="ends",
    )(slab, face, inverse, *planes)


def finish_kernel(
    chunks, slab_ref, face_ref, inverse_ref, carry_ref, ends_ref, weight_x, weight_y, *rest
):
    planes, outs = rest[:chunks], rest[chunks:]
    slab_depth, rows, m = inverse_ref.shape
    depth = slab_depth // chunks
    slabs = carry_ref.shape[0]
    slab = slab_ref[0]
    zero = jnp.zeros((rows, m), f32)
    rising = [zero]
    for group in range(slabs - 1):
        rising.append(ends_ref[group, 0] + carry_ref[group, 0] * rising[-1])
    entering = zero
    for group in range(1, slabs):
        entering = jnp.where(slab == group, rising[group], entering)
    leaving = zero
    value = None
    for group in reversed(range(1, slabs)):
        first = ends_ref[group, 1] + carry_ref[group, 1] * rising[group]
        value = first if value is None else first + carry_ref[group, 2] * value
        leaving = jnp.where(slab == group - 1, value, leaving)
    faces = slab_faces(slab_ref, face_ref, slab_depth)
    solved, _ = sweep(planes, inverse_ref, faces, entering, leaving, m, depth)
    weight = weight_x[...] * weight_y[...]
    for place in range(slab_depth):
        at = place % depth
        outs[place // depth][:, at * m : (at + 1) * m] = solved[place] * weight


def finish(slab, face, inverse, carry, gathered, weight_x, weight_y, planes):
    slab_depth, length, m = inverse.shape
    chunks = len(planes)
    slabs = carry.shape[0]
    rows = min(128, length)
    plane_specs = [pl.BlockSpec((rows, plane.shape[1]), lambda i: (i, 0)) for plane in planes]
    return pl.pallas_call(
        functools.partial(finish_kernel, chunks),
        out_shape=tuple(jax.ShapeDtypeStruct(plane.shape, f32) for plane in planes),
        grid=(length // rows,),
        in_specs=[
            smem(),
            smem(),
            pl.BlockSpec((slab_depth, rows, m), lambda i: (0, i, 0)),
            pl.BlockSpec((slabs, 3, rows, m), lambda i: (0, 0, i, 0)),
            pl.BlockSpec((slabs, 2, rows, m), lambda i: (0, 0, i, 0)),
            pl.BlockSpec((rows, 1), lambda i: (i, 0)),
            pl.BlockSpec((1, m), lambda i: (0, 0)),
        ]
        + plane_specs,
        out_specs=tuple(plane_specs),
        compiler_params=params(),
        cost_estimate=cost(
            8 * slab_depth * length * m, 4 * length * m * (3 * slab_depth + 5 * slabs)
        ),
        name="finish",
    )(slab, face, inverse, carry, gathered, weight_x, weight_y, *planes)


def body(charge, cell_permittivity, face_permittivity, screening):
    slab_depth, x_local, width_y = charge.shape
    groups = lax.axis_size("gx")
    width_x = x_local * groups
    m = width_y // groups
    depth = min(slab_depth, max(1, LANES // m))
    chunks = slab_depth // depth
    table_y = basis_table(width_y)
    table_x = basis_table(width_x)
    y_high, y_low = (jnp.asarray(part) for part in halves(table_y))
    yt_high, yt_low = (jnp.asarray(part) for part in halves(np.ascontiguousarray(table_y.T)))
    if width_x == width_y:
        x_high, x_low, xt_high, xt_low = y_high, y_low, yt_high, yt_low
    else:
        x_high, x_low = (jnp.asarray(part) for part in halves(table_x))
        xt_high, xt_low = (jnp.asarray(part) for part in halves(np.ascontiguousarray(table_x.T)))
    place = lax.axis_index("gx") * m
    shift_x = jnp.asarray(mode_shift(width_x)[:, None])
    weight_x = jnp.asarray(mode_weights(width_x)[:, None])
    shift_y = lax.dynamic_slice_in_dim(jnp.asarray(mode_shift(width_y)[None]), place, m, 1)
    weight_y = lax.dynamic_slice_in_dim(jnp.asarray(mode_weights(width_y)[None]), place, m, 1)
    slab = lax.axis_index("gz").astype(jnp.int32).reshape(1)

    exchange = functools.partial(
        lax.all_to_all, axis_name="gx", split_axis=0, concat_axis=0, tiled=True
    )
    inverse, carry = pivots(
        slab, cell_permittivity, face_permittivity, screening, shift_x, shift_y, slab_depth
    )
    planes = []
    for chunk in range(chunks):
        sent = forward_y(charge, chunk, depth, y_high, y_low, groups)
        got = exchange(sent).reshape(width_x, depth * m)
        planes.append(left_multiply(xt_high, xt_low, got, "forward_x"))
    own_ends = ends(slab, face_permittivity, inverse, planes)
    gathered = lax.all_gather(own_ends, "gz", axis=0)
    solved = finish(
        slab, face_permittivity, inverse, carry, gathered, weight_x, weight_y, planes
    )
    result = None
    for chunk in range(chunks):
        sent = left_multiply(x_high, x_low, solved[chunk], "back_x")
        got = exchange(sent.reshape(groups, x_local, depth * m))
        result = back_y(got, chunk, depth, slab_depth, yt_high, yt_low, result)
    return result


def solution(mesh):
    in_specs = (P("gz", "gx", None), P(), P(), P())
    out_specs = P("gz", "gx", None)
    return jax.shard_map(body, mesh=mesh, in_specs=in_specs, out_specs=out_specs, check_vma=False)
```

```python
import functools

import jax
import jax.numpy as jnp
import ml_dtypes
import numpy as np
from jax import lax
from jax.experimental import pallas as pl
from jax.experimental.pallas import tpu as pltpu
from jax.sharding import PartitionSpec as P

f32 = jnp.float32
bf16 = jnp.bfloat16
LANES = 128
ROWS = 8
STEP = 16
CHUNKS = 2


def params():
    return pltpu.CompilerParams(
        vmem_limit_bytes=48 * 1024 * 1024, dimension_semantics=("arbitrary",)
    )


def cost(flops, moved):
    return pl.CostEstimate(flops=flops, bytes_accessed=moved, transcendentals=0)


def frequencies(length):
    col = np.arange(length)
    middle = length // 2
    return np.where(col <= middle, col, col - middle)


def basis_table(length):
    freq = frequencies(length)
    phase = (np.arange(length)[:, None] * freq[None, :]) % length
    angles = phase * (2.0 * np.pi / length)
    cos_part = np.arange(length)[None, :] <= length // 2
    return np.where(cos_part, np.cos(angles), np.sin(angles))


def halves(table):
    high = table.astype(ml_dtypes.bfloat16)
    low = (table - high.astype(np.float64)).astype(ml_dtypes.bfloat16)
    return jnp.asarray(high), jnp.asarray(low)


def mode_weights(length):
    col = np.arange(length)
    edge = (col == 0) | (col == length // 2)
    return np.where(edge, 1.0 / length, 2.0 / length)


def mode_shift(length):
    return (2.0 - 2.0 * np.cos(frequencies(length) * (2.0 * np.pi / length))).astype(np.float32)


def split(value):
    high = value.astype(bf16)
    low = (value - high.astype(f32)).astype(bf16)
    return high, low


def product(left, right):
    dot = functools.partial(jnp.dot, preferred_element_type=f32)
    return dot(left[0], right[0]) + (dot(left[0], right[1]) + dot(left[1], right[0]))


def eigen_kernel(
    cell_col, cell_row, face_col, face_row, low_row, screen_col, screen_row, shift_row,
    ratio_ref, fore_high, fore_low, back_high, back_low,
):
    n = cell_col.shape[0]
    shape = (n, LANES)
    row = lax.broadcasted_iota(jnp.int32, shape, 0)
    col = lax.broadcasted_iota(jnp.int32, shape, 1)
    lane = lax.broadcasted_iota(jnp.int32, (1, LANES), 1)
    unit = (row == col).astype(f32)

    def pairing(parity):
        def lower(index):
            return ((index + parity) % 2 == 0) & (index < n - 1)

        def upper(index):
            return ((index + parity) % 2 == 1) & (index > 0) & (index < n)

        mate = jnp.where(lower(col), col + 1, jnp.where(upper(col), col - 1, -1))
        return (
            (row == mate).astype(f32),
            lower(col),
            lower(row),
            lower(lane),
            lower(lane) | upper(lane),
        )

    pairings = (pairing(0), pairing(1))

    def lane_mates(value, low):
        return jnp.where(low, pltpu.roll(value, LANES - 1, 1), pltpu.roll(value, 1, 1))

    def stage(matrix, vectors, pair):
        mate, low_cols, low_rows, low_lane, paired = pair
        other = lane_mates(matrix, low_cols)
        gap = jnp.sum(mate * other - unit * matrix, axis=0, keepdims=True)
        twice = jnp.sum(mate * matrix + unit * other, axis=0, keepdims=True)
        positive = (gap > 0.0) | ((gap == 0.0) & low_lane)
        size = jnp.abs(gap) + jnp.sqrt(gap * gap + twice * twice) + 1e-30
        tangent = jnp.where(positive, twice, -twice) / size
        square = 1.0 + tangent * tangent
        cosine = lax.rsqrt(square)
        cosine = cosine * (1.5 - 0.5 * square * cosine * cosine)
        own = jnp.where(paired, cosine * tangent, 1.0)
        cross = jnp.where(paired, cosine, 0.0)
        own_col = jnp.sum(unit * own, axis=1, keepdims=True)
        cross_col = jnp.sum(unit * cross, axis=1, keepdims=True)
        vectors = vectors * own + lane_mates(vectors, low_cols) * cross
        matrix = matrix * own + other * cross
        other = jnp.where(low_rows, pltpu.roll(matrix, n - 1, 0), pltpu.roll(matrix, 1, 0))
        return matrix * own_col + other * cross_col, vectors

    scale_col = 1.0 / jnp.sqrt(cell_col[...])
    scale_row = 1.0 / jnp.sqrt(cell_row[...])
    tri = (
        unit * (low_row[...] + face_row[...] + screen_row[...])
        - (col == row + 1).astype(f32) * face_col[...]
        - ((col == row - 1) & (row < n)).astype(f32) * face_row[...]
    )
    matrix = scale_col * tri * scale_row
    whole = jnp.sum(matrix * matrix)

    def unsettled(state):
        sweep, off, _, _ = state
        return (sweep < 15) & (off > 1e-10 * whole)

    def one_sweep(state):
        sweep, _, matrix, vectors = state

        def two(_, held):
            held = stage(held[0], held[1], pairings[0])
            return stage(held[0], held[1], pairings[1])

        matrix, vectors = lax.fori_loop(0, n // 2, two, (matrix, vectors))
        rest = matrix * (1.0 - unit)
        return sweep + 1, jnp.sum(rest * rest), matrix, vectors

    _, _, _, vectors = lax.while_loop(
        unsettled, one_sweep, (jnp.int32(0), whole, matrix, unit)
    )
    modes = scale_col * vectors
    norm = jnp.sum(cell_col[...] * modes * modes, axis=0, keepdims=True)
    modes = modes * (1.0 / jnp.sqrt(jnp.where(lane < n, norm, 1.0)))
    rise = pltpu.roll(modes, n - 1, 0) - modes
    walls = jnp.where((row == 0) | (row == n - 1), 1.0, 0.0) * face_col[n - 1 : n, :]
    energy = (screen_col[...] + walls) * modes * modes
    energy = energy + jnp.where(row < n - 1, face_col[...], 0.0) * rise * rise
    values = jnp.sum(energy, axis=0, keepdims=True)
    total = jnp.sum(unit * values, axis=1, keepdims=True) + shift_row[...]
    ratio_ref[...] = 2.0 / (2.0 + total + jnp.sqrt(total * (total + 4.0)))

    size = ROWS * n

    def flags(shape, test):
        first = lax.broadcasted_iota(jnp.int32, shape, 0)
        second = lax.broadcasted_iota(jnp.int32, shape, 1)
        return jnp.where(test(first, second), 1.0, 0.0)

    pick_mode = flags((size, LANES), lambda a, b: a % n == b).astype(bf16)
    pick_layer = flags((size, n), lambda a, b: a // ROWS == b).astype(bf16)
    spread_layer = flags((n, size), lambda a, b: b // ROWS == a).astype(bf16)
    same_fore = flags((size, size), lambda a, b: a // n == b % ROWS)
    same_back = flags((size, size), lambda a, b: a % ROWS == b // n)
    across = (((1,), (1,)), ((), ()))
    for part, fore, back in zip(split(modes), (fore_high, fore_low), (back_high, back_low)):
        turned = lax.dot_general(pick_mode, part, across, preferred_element_type=f32)
        spread = jnp.dot(turned.astype(bf16), spread_layer, preferred_element_type=f32)
        fore[...] = (spread * same_fore).astype(bf16)
        layered = jnp.dot(pick_layer, part, preferred_element_type=f32)
        spread = lax.dot_general(
            layered.astype(bf16), pick_mode, across, preferred_element_type=f32
        )
        back[...] = (spread * same_back).astype(bf16)


def eigen(cell, face, screening, shift_row):
    n = cell.shape[0]
    size = ROWS * n

    def as_row(value):
        return jnp.pad(value, (0, LANES - n), constant_values=1.0)[None]

    table = jax.ShapeDtypeStruct((size, size), bf16)
    return pl.pallas_call(
        eigen_kernel,
        out_shape=(jax.ShapeDtypeStruct((n, shift_row.shape[1]), f32),) + (table,) * 4,
        compiler_params=pltpu.CompilerParams(vmem_limit_bytes=32 * 1024 * 1024),
        cost_estimate=cost(20_000_000_000, 4 * size * size),
        name="eigen",
    )(
        cell[:, None], as_row(cell), face[:, None], as_row(face), as_row(jnp.roll(face, 1)),
        screening[:, None], as_row(screening), shift_row,
    )


def forward_y_kernel(charge_ref, high_ref, low_ref, out_ref, rows_high, rows_low):
    @pl.when(pl.program_id(0) == 0)
    def _():
        high, low = split(charge_ref[...].reshape(rows_high.shape))
        rows_high[...] = high
        rows_low[...] = low

    result = product((rows_high[...], rows_low[...]), (high_ref[...], low_ref[...]))
    out_ref[...] = result.reshape(out_ref.shape)


def forward_y(charge, chunk, high, low, slabs):
    depth, x_local, width = charge.shape
    rows = x_local // CHUNKS
    part = width // slabs
    return pl.pallas_call(
        forward_y_kernel,
        out_shape=jax.ShapeDtypeStruct((slabs, depth, rows, part), f32),
        grid=(slabs,),
        in_specs=[
            pl.BlockSpec((depth, rows, width), lambda i: (0, chunk, 0)),
            pl.BlockSpec((width, part), lambda i: (0, i)),
            pl.BlockSpec((width, part), lambda i: (0, i)),
        ],
        out_specs=pl.BlockSpec((1, depth, rows, part), lambda i: (i, 0, 0, 0)),
        scratch_shapes=[pltpu.VMEM((depth * rows, width), bf16)] * 2,
        compiler_params=params(),
        cost_estimate=cost(6 * depth * rows * width * width, 4 * width * width),
        name="forward_y",
    )(charge, high, low)


def rise_kernel(first, value_ref, high_ref, low_ref, ratio_ref, *rest):
    if first:
        out_ref, ends_ref, power_ref = rest
    else:
        ends_in, power_in, out_ref, ends_ref, power_ref = rest
    layers, _, part = value_ref.shape

    @pl.when(pl.program_id(0) == 0)
    def _():
        if first:
            ends_ref[...] = jnp.zeros_like(ends_ref)
            power_ref[...] = ratio_ref[...]
        else:
            ends_ref[...] = ends_in[...]
            power_ref[...] = power_in[...]

    ratio = ratio_ref[...]
    for start in range(0, STEP, ROWS):
        block = value_ref[:, start : start + ROWS, :].reshape(layers * ROWS, part)
        modes = product((high_ref[...], low_ref[...]), split(block))
        value, total, power = ends_ref[0], ends_ref[1], power_ref[...]
        for x in range(ROWS):
            value = modes[x * layers : (x + 1) * layers] + ratio * value
            out_ref[start + x] = value
            total = total + power * value
            power = power * ratio
        ends_ref[0] = value
        ends_ref[1] = total
        power_ref[...] = power


def rise(value, high, low, ratio, state):
    layers, rows, part = value.shape
    table = pl.BlockSpec(high.shape, lambda i: (0, 0))
    plane = pl.BlockSpec((layers, part), lambda i: (0, 0))
    pair = pl.BlockSpec((2, layers, part), lambda i: (0, 0, 0))
    return pl.pallas_call(
        functools.partial(rise_kernel, state is None),
        out_shape=(
            jax.ShapeDtypeStruct((rows, layers, part), f32),
            jax.ShapeDtypeStruct((2, layers, part), f32),
            jax.ShapeDtypeStruct((layers, part), f32),
        ),
        grid=(rows // STEP,),
        in_specs=[pl.BlockSpec((layers, STEP, part), lambda i: (0, i, 0)), table, table, plane]
        + ([] if state is None else [pair, plane]),
        out_specs=(pl.BlockSpec((STEP, layers, part), lambda i: (i, 0, 0)), pair, plane),
        compiler_params=params(),
        cost_estimate=cost(6 * ROWS * layers * layers * rows * part, 8 * rows * layers * part),
        name="rise",
    )(value, high, low, ratio, *(() if state is None else state))


def link_kernel(x_local, place_ref, ratio_ref, ends_ref, enter_ref, leave_ref):
    blocks = ends_ref.shape[0]
    place = place_ref[0]
    ratio = ratio_ref[...]

    def raised(base, count):
        value = None
        while count:
            if count & 1:
                value = base if value is None else value * base
            base = base * base
            count >>= 1
        return value

    across = raised(ratio, x_local)
    around = 1.0 / (1.0 - raised(across, blocks))
    both = ratio * ratio * (1.0 - across * across) / ((1.0 - ratio) * (1.0 + ratio))
    last = ends_ref[0, 0]
    for block in range(1, blocks):
        last = ends_ref[block, 0] + across * last
    last = last * around
    tops = []
    enter = jnp.zeros_like(last)
    for block in range(blocks):
        enter = jnp.where(place == block, last, enter)
        tops.append(ends_ref[block, 1] + both * last)
        last = ends_ref[block, 0] + across * last
    enter_ref[...] = enter
    first = tops[-1]
    for block in reversed(range(blocks - 1)):
        first = tops[block] + across * first
    first = first * around
    leave = jnp.zeros_like(first)
    for block in reversed(range(blocks)):
        leave = jnp.where(place == block, first, leave)
        first = tops[block] + across * first
    leave_ref[...] = leave


def link(place, ratio, gathered, x_local):
    plane = jax.ShapeDtypeStruct(ratio.shape, f32)
    vmem = pl.BlockSpec(memory_space=pltpu.VMEM)
    return pl.pallas_call(
        functools.partial(link_kernel, x_local),
        out_shape=(plane, plane),
        in_specs=[pl.BlockSpec(memory_space=pltpu.SMEM), vmem, vmem],
        out_specs=(vmem, vmem),
        cost_estimate=cost(10 * gathered.size, 4 * gathered.size),
        name="link",
    )(place, ratio, gathered)


def fall_kernel(
    first_row, value_ref, high_ref, low_ref, ratio_ref, enter_ref, leave_ref,
    out_ref, carry_ref, near_ref, far_ref, held_ref,
):
    layers, _, part = out_ref.shape
    ratio = ratio_ref[...]

    @pl.when(pl.program_id(0) == 0)
    def _():
        carry_ref[...] = leave_ref[...]
        power = ratio
        for x in range(ROWS):
            near_ref[x] = power
            if x < ROWS - 1:
                power = power * ratio
        value = enter_ref[...]
        for block in range(far_ref.shape[0]):
            far_ref[block] = value
            value = value * power

    step = pl.num_programs(0) - 1 - pl.program_id(0)
    value = carry_ref[...]
    for start in reversed(range(0, STEP, ROWS)):
        far = far_ref[(first_row + start) // ROWS + step * (STEP // ROWS)]
        for x in reversed(range(ROWS)):
            value = ratio * (value_ref[start + x] + near_ref[x] * far + value)
            held_ref[x * layers : (x + 1) * layers] = value
        solved = product((high_ref[...], low_ref[...]), split(held_ref[...]))
        out_ref[:, start : start + ROWS, :] = solved.reshape(layers, ROWS, part)
    carry_ref[...] = value


def fall(value, chunk, x_local, high, low, ratio, enter, leave):
    rows, layers, part = value.shape
    steps = rows // STEP
    table = pl.BlockSpec(high.shape, lambda i: (0, 0))
    plane = pl.BlockSpec((layers, part), lambda i: (0, 0))
    return pl.pallas_call(
        functools.partial(fall_kernel, chunk * rows),
        out_shape=(
            jax.ShapeDtypeStruct((layers, rows, part), f32),
            jax.ShapeDtypeStruct((layers, part), f32),
        ),
        grid=(steps,),
        in_specs=[
            pl.BlockSpec((STEP, layers, part), lambda i: (steps - 1 - i, 0, 0)),
            table, table, plane, plane, plane,
        ],
        out_specs=(
            pl.BlockSpec((layers, STEP, part), lambda i: (0, steps - 1 - i, 0)),
            plane,
        ),
        scratch_shapes=[
            pltpu.VMEM((ROWS, layers, part), f32),
            pltpu.VMEM((x_local // ROWS, layers, part), f32),
            pltpu.VMEM((ROWS * layers, part), f32),
        ],
        compiler_params=params(),
        cost_estimate=cost(6 * ROWS * layers * layers * rows * part, 8 * rows * layers * part),
        name="fall",
    )(value, high, low, ratio, enter, leave)


def back_y_kernel(value_ref, high_ref, low_ref, *rest):
    out_ref, rows_high, rows_low = rest[-3:]
    slabs, depth, rows, part = value_ref.shape

    @pl.when(pl.program_id(0) == 0)
    def _():
        for slab in range(slabs):
            high, low = split(value_ref[slab].reshape(depth * rows, part))
            rows_high[:, slab * part : (slab + 1) * part] = high
            rows_low[:, slab * part : (slab + 1) * part] = low

    result = product((rows_high[...], rows_low[...]), (high_ref[...], low_ref[...]))
    out_ref[...] = result.reshape(out_ref.shape)


def back_y(value, chunk, x_local, high, low, held):
    _, depth, rows, _ = value.shape
    width = high.shape[0]
    columns = min(256, width)
    operands = [value, high, low]
    in_specs = [
        pl.BlockSpec(value.shape, lambda i: (0, 0, 0, 0)),
        pl.BlockSpec((width, columns), lambda i: (0, i)),
        pl.BlockSpec((width, columns), lambda i: (0, i)),
    ]
    aliases = {}
    if held is not None:
        operands.append(held)
        in_specs.append(pl.BlockSpec(memory_space=pl.ANY))
        aliases = {3: 0}
    return pl.pallas_call(
        back_y_kernel,
        out_shape=jax.ShapeDtypeStruct((depth, x_local, width), f32),
        grid=(width // columns,),
        in_specs=in_specs,
        out_specs=pl.BlockSpec((depth, rows, columns), lambda i: (0, chunk, i)),
        scratch_shapes=[pltpu.VMEM((depth * rows, width), bf16)] * 2,
        input_output_aliases=aliases,
        compiler_params=params(),
        cost_estimate=cost(6 * depth * rows * width * width, 4 * width * width),
        name="back_y",
    )(*operands)


def body(charge, cell_permittivity, face_permittivity, screening):
    depth, x_local, width = charge.shape
    slabs = lax.axis_size("gz")
    layers = depth * slabs
    rows = x_local // CHUNKS
    part = width // slabs
    table = basis_table(width)
    fore_high, fore_low = halves(table * mode_weights(width)[None, :])
    back_high, back_low = halves(np.ascontiguousarray(table.T))
    shift_row = lax.dynamic_slice_in_dim(
        jnp.asarray(mode_shift(width)[None]), lax.axis_index("gz") * part, part, 1
    )
    place = lax.axis_index("gx").astype(jnp.int32).reshape(1)
    exchange = functools.partial(
        lax.all_to_all, axis_name="gz", split_axis=0, concat_axis=0, tiled=True
    )
    ratio, to_high, to_low, from_high, from_low = eigen(
        cell_permittivity, face_permittivity, screening, shift_row
    )
    state = None
    risen = []
    for chunk in range(CHUNKS):
        sent = forward_y(charge, chunk, fore_high, fore_low, slabs)
        got = exchange(sent).reshape(layers, rows, part)
        value, *state = rise(got, to_high, to_low, ratio, state)
        risen.append(value)
    gathered = lax.all_gather(state[0], "gx", axis=0)
    enter, leave = link(place, ratio, gathered, x_local)
    result = None
    for chunk in reversed(range(CHUNKS)):
        sent, leave = fall(
            risen[chunk], chunk, x_local, from_high, from_low, ratio, enter, leave
        )
        got = exchange(sent.reshape(slabs, depth, rows, part))
        result = back_y(got, chunk, x_local, back_high, back_low, result)
    return result


def solution(mesh):
    in_specs = (P("gz", "gx", None), P(), P(), P())
    out_specs = P("gz", "gx", None)
    return jax.shard_map(body, mesh=mesh, in_specs=in_specs, out_specs=out_specs, check_vma=False)
```

```python
import functools

import jax
import jax.numpy as jnp
import ml_dtypes
import numpy as np
from jax import lax
from jax.experimental import pallas as pl
from jax.experimental.pallas import tpu as pltpu
from jax.sharding import PartitionSpec as P

f32 = jnp.float32
bf16 = jnp.bfloat16
LANES = 128
VMEM = 60 * 1024 * 1024
MESH = pl.DeviceIdType.MESH
ROWS = 8
STEP = 16
CHUNKS = 2


def params():
    return pltpu.CompilerParams(
        vmem_limit_bytes=VMEM, dimension_semantics=("arbitrary",)
    )


def cost(flops, moved):
    return pl.CostEstimate(flops=flops, bytes_accessed=moved, transcendentals=0)


def frequencies(length):
    col = np.arange(length)
    middle = length // 2
    return np.where(col <= middle, col, col - middle)


def basis_table(length):
    freq = frequencies(length)
    phase = (np.arange(length)[:, None] * freq[None, :]) % length
    angles = phase * (2.0 * np.pi / length)
    cos_part = np.arange(length)[None, :] <= length // 2
    return np.where(cos_part, np.cos(angles), np.sin(angles))


def halves(table):
    high = table.astype(ml_dtypes.bfloat16)
    low = (table - high.astype(np.float64)).astype(ml_dtypes.bfloat16)
    return jnp.asarray(high), jnp.asarray(low)


def mode_weights(length):
    col = np.arange(length)
    edge = (col == 0) | (col == length // 2)
    return np.where(edge, 1.0 / length, 2.0 / length)


def mode_shift(length):
    return (2.0 - 2.0 * np.cos(frequencies(length) * (2.0 * np.pi / length))).astype(np.float32)


def split(value):
    high = value.astype(bf16)
    low = (value - high.astype(f32)).astype(bf16)
    return high, low


def product(left, right):
    dot = functools.partial(jnp.dot, preferred_element_type=f32)
    return dot(left[0], right[0]) + (dot(left[0], right[1]) + dot(left[1], right[0]))


def one_stage(held, pair):
    n = held.shape[0]
    unit, mate, low_cols, low_rows, paired_cols, paired_rows = pair

    def lane_mates(value):
        return jnp.where(low_cols, pltpu.roll(value, LANES - 1, 1), pltpu.roll(value, 1, 1))

    def row_mates(value):
        return jnp.where(low_rows, pltpu.roll(value, n - 1, 0), pltpu.roll(value, 1, 0))

    def rotation(other, axis, low, paired):
        gap = jnp.sum(mate * other - unit * held, axis=axis, keepdims=True)
        twice = jnp.sum(mate * held + unit * other, axis=axis, keepdims=True)
        square = jnp.maximum(gap * gap + twice * twice, 1e-35)
        inverse = lax.rsqrt(square)
        inverse = inverse * (1.5 - 0.5 * square * inverse * inverse)
        half = 0.5 + 0.5 * jnp.abs(gap) * inverse
        root = lax.rsqrt(half)
        root = root * (1.5 - 0.5 * half * root * root)
        positive = (gap > 0.0) | ((gap == 0.0) & low)
        sine = 0.5 * jnp.where(positive, twice, -twice) * inverse * root
        return jnp.where(paired, sine, 1.0), jnp.where(paired, half * root, 0.0)

    by_lane = lane_mates(held)
    by_row = row_mates(held)
    by_both = row_mates(by_lane)
    own_row, cross_row = rotation(by_lane, 0, low_cols[:1], paired_cols[:1])
    own_col, cross_col = rotation(by_row, 1, low_rows[:, :1], paired_rows[:, :1])
    return own_col * (own_row * held + cross_row * by_lane) + cross_col * (
        own_row * by_row + cross_row * by_both
    )


def pairings(n):
    shape = (n, LANES)
    row = lax.broadcasted_iota(jnp.int32, shape, 0)
    col = lax.broadcasted_iota(jnp.int32, shape, 1)
    unit = (row == col).astype(f32)

    def pairing(parity):
        def lower(index):
            return ((index + parity) % 2 == 0) & (index < n - 1)

        def upper(index):
            return ((index + parity) % 2 == 1) & (index > 0) & (index < n)

        mate = jnp.where(lower(col), col + 1, jnp.where(upper(col), col - 1, -1))
        return (
            unit,
            (row == mate).astype(f32),
            lower(col),
            lower(row),
            lower(col) | upper(col),
            lower(row) | upper(row),
        )

    return pairing(0), pairing(1)


def one_sweep(held, pairs):
    def two(_, value):
        return one_stage(one_stage(value, pairs[0]), pairs[1])

    return lax.fori_loop(0, held.shape[0] // 2, two, held)


def begin_kernel(
    sweeps, cell_col, cell_row, face_col, face_row, low_row, screen_row, after_ref, held_ref
):
    n = cell_col.shape[0]
    row = lax.broadcasted_iota(jnp.int32, held_ref.shape, 0)
    col = lax.broadcasted_iota(jnp.int32, held_ref.shape, 1)
    tri = (
        (row == col).astype(f32) * (low_row[...] + face_row[...] + screen_row[...])
        - (col == row + 1).astype(f32) * face_col[...]
        - (col == row - 1).astype(f32) * face_row[...]
    )
    matrix = tri * (1.0 / jnp.sqrt(cell_col[...])) * (1.0 / jnp.sqrt(cell_row[...]))
    held = jnp.where(col < n, matrix, (col == row + n).astype(f32))
    pairs = pairings(n)
    held_ref[...] = lax.fori_loop(0, sweeps, lambda _, value: one_sweep(value, pairs), held)


def end_kernel(
    held_ref, cell_row, face_row, screen_row, shift_row, after_ref,
    ratio_ref, fore_high, fore_low, back_high, back_low,
):
    n = held_ref.shape[0]
    row = lax.broadcasted_iota(jnp.int32, held_ref.shape, 0)
    col = lax.broadcasted_iota(jnp.int32, held_ref.shape, 1)
    diagonal = row == col
    beside = (col < n) & (row != col)
    pairs = pairings(n)

    def unsettled(state):
        sweep, off, whole, _ = state
        return (sweep < 15) & (off > 1e-10 * whole)

    def sweep_on(state):
        sweep, _, _, held = state
        held = one_sweep(held, pairs)
        return sweep + 1, *sizes(held), held

    def sizes(held):
        square = held * held
        return jnp.sum(jnp.where(beside, square, 0.0)), jnp.sum(jnp.where(diagonal, square, 0.0))

    held = held_ref[...]
    held = lax.while_loop(unsettled, sweep_on, (jnp.int32(0), *sizes(held), held))[3]
    layer = col < n
    modes = jnp.where(layer, pltpu.roll(held, LANES - n, 1), 0.0) / jnp.sqrt(cell_row[...])
    norm = jnp.sum(cell_row[...] * modes * modes, axis=1, keepdims=True)
    modes = modes * (1.0 / jnp.sqrt(norm))
    slope = pltpu.roll(modes, LANES - 1, 1) - modes
    wall = face_row[:, n - 1 : n]
    walls = jnp.where((col == 0) | (col == n - 1), 1.0, 0.0) * wall
    energy = (screen_row[...] + walls) * modes * modes
    energy = energy + jnp.where(col < n - 1, face_row[...], 0.0) * slope * slope
    values = jnp.sum(energy, axis=1, keepdims=True)
    total = values + shift_row[...]
    ratio_ref[...] = 2.0 / (2.0 + total + jnp.sqrt(total * (total + 4.0)))

    size = ROWS * n

    def flags(shape, test):
        first = lax.broadcasted_iota(jnp.int32, shape, 0)
        second = lax.broadcasted_iota(jnp.int32, shape, 1)
        return jnp.where(test(first, second), 1.0, 0.0)

    pick_mode = flags((size, n), lambda a, b: a % n == b).astype(bf16)
    spread_mode = flags((n, size), lambda a, b: b % n == a).astype(bf16)
    pick_layer = flags((size, LANES), lambda a, b: a // ROWS == b).astype(bf16)
    spread_layer = flags((LANES, size), lambda a, b: b // ROWS == a).astype(bf16)
    same_fore = flags((size, size), lambda a, b: a // n == b % ROWS)
    same_back = flags((size, size), lambda a, b: a % ROWS == b // n)
    across = (((1,), (1,)), ((), ()))
    for part, fore, back in zip(split(modes), (fore_high, fore_low), (back_high, back_low)):
        turned = jnp.dot(pick_mode, part, preferred_element_type=f32)
        spread = jnp.dot(turned.astype(bf16), spread_layer, preferred_element_type=f32)
        fore[...] = (spread * same_fore).astype(bf16)
        layered = lax.dot_general(pick_layer, part, across, preferred_element_type=f32)
        spread = jnp.dot(layered.astype(bf16), spread_mode, preferred_element_type=f32)
        back[...] = (spread * same_back).astype(bf16)


def as_row(value):
    return jnp.pad(value, (0, LANES - value.shape[0]), constant_values=1.0)[None]


def eigen_begin(cell, face, screening, after):
    n = cell.shape[0]
    vmem = pl.BlockSpec(memory_space=pltpu.VMEM)
    return pl.pallas_call(
        functools.partial(begin_kernel, 2),
        out_shape=jax.ShapeDtypeStruct((n, LANES), f32),
        in_specs=[vmem] * 6 + [pl.BlockSpec(memory_space=pl.ANY)],
        out_specs=vmem,
        compiler_params=pltpu.CompilerParams(vmem_limit_bytes=VMEM),
        cost_estimate=cost(10_000_000_000, 4 * n * LANES),
        name="eigen_begin",
    )(
        cell[:, None], as_row(cell), face[:, None], as_row(face), as_row(jnp.roll(face, 1)),
        as_row(screening), after,
    )


def eigen_end(held, cell, face, screening, shift_row, after):
    n = cell.shape[0]
    size = ROWS * n
    table = jax.ShapeDtypeStruct((size, size), bf16)
    vmem = pl.BlockSpec(memory_space=pltpu.VMEM)
    return pl.pallas_call(
        end_kernel,
        out_shape=(jax.ShapeDtypeStruct((n, shift_row.shape[1]), f32),) + (table,) * 4,
        in_specs=[vmem] * 5 + [pl.BlockSpec(memory_space=pl.ANY)],
        out_specs=(vmem,) * 5,
        compiler_params=pltpu.CompilerParams(vmem_limit_bytes=VMEM),
        cost_estimate=cost(15_000_000_000, 4 * size * size),
        name="eigen_end",
    )(held, as_row(cell), as_row(face), as_row(screening), shift_row, after)


def forward_y_kernel(charge_ref, high_ref, low_ref, after_ref, out_ref, rows_high, rows_low):
    @pl.when(pl.program_id(0) == 0)
    def _():
        high, low = split(charge_ref[...].reshape(rows_high.shape))
        rows_high[...] = high
        rows_low[...] = low

    result = product((rows_high[...], rows_low[...]), (high_ref[...], low_ref[...]))
    out_ref[...] = result.reshape(out_ref.shape)


def forward_y(charge, chunk, high, low, slabs, after):
    depth, x_local, width = charge.shape
    rows = x_local // CHUNKS
    part = width // slabs
    return pl.pallas_call(
        forward_y_kernel,
        out_shape=jax.ShapeDtypeStruct((slabs, depth, rows, part), f32),
        grid=(slabs,),
        in_specs=[
            pl.BlockSpec((depth, rows, width), lambda i: (0, chunk, 0)),
            pl.BlockSpec((width, part), lambda i: (0, i)),
            pl.BlockSpec((width, part), lambda i: (0, i)),
            pl.BlockSpec(memory_space=pl.ANY),
        ],
        out_specs=pl.BlockSpec((1, depth, rows, part), lambda i: (i, 0, 0, 0)),
        scratch_shapes=[pltpu.VMEM((depth * rows, width), bf16)] * 2,
        compiler_params=params(),
        cost_estimate=cost(6 * depth * rows * width * width, 4 * width * width),
        name="forward_y",
    )(charge, high, low, after)


def rise_kernel(first, value_ref, high_ref, low_ref, ratio_ref, *rest):
    if first:
        out_ref, ends_ref, power_ref = rest
    else:
        ends_in, power_in, out_ref, ends_ref, power_ref = rest
    layers, _, part = value_ref.shape

    @pl.when(pl.program_id(0) == 0)
    def _():
        if first:
            ends_ref[...] = jnp.zeros_like(ends_ref)
            power_ref[...] = ratio_ref[...]
        else:
            ends_ref[...] = ends_in[...]
            power_ref[...] = power_in[...]

    ratio = ratio_ref[...]
    for start in range(0, STEP, ROWS):
        block = value_ref[:, start : start + ROWS, :].reshape(layers * ROWS, part)
        modes = product((high_ref[...], low_ref[...]), split(block))
        value, total, power = ends_ref[0], ends_ref[1], power_ref[...]
        for x in range(ROWS):
            value = modes[x * layers : (x + 1) * layers] + ratio * value
            out_ref[start + x] = value
            total = total + power * value
            power = power * ratio
        ends_ref[0] = value
        ends_ref[1] = total
        power_ref[...] = power


def rise(value, high, low, ratio, state):
    layers, rows, part = value.shape
    table = pl.BlockSpec(high.shape, lambda i: (0, 0))
    plane = pl.BlockSpec((layers, part), lambda i: (0, 0))
    pair = pl.BlockSpec((2, layers, part), lambda i: (0, 0, 0))
    return pl.pallas_call(
        functools.partial(rise_kernel, state is None),
        out_shape=(
            jax.ShapeDtypeStruct((rows, layers, part), f32),
            jax.ShapeDtypeStruct((2, layers, part), f32),
            jax.ShapeDtypeStruct((layers, part), f32),
        ),
        grid=(rows // STEP,),
        in_specs=[pl.BlockSpec((layers, STEP, part), lambda i: (0, i, 0)), table, table, plane]
        + ([] if state is None else [pair, plane]),
        out_specs=(pl.BlockSpec((STEP, layers, part), lambda i: (i, 0, 0)), pair, plane),
        compiler_params=params(),
        cost_estimate=cost(6 * ROWS * layers * layers * rows * part, 8 * rows * layers * part),
        name="rise",
    )(value, high, low, ratio, *(() if state is None else state))


def link_kernel(
    x_local, ratio_ref, ends_ref, enter_ref, leave_ref, held_ref, send_sems, recv_sems
):
    blocks = held_ref.shape[0]
    me = lax.axis_index("gx")
    barrier = pltpu.get_barrier_semaphore()
    for step in range(1, blocks):
        other = lax.rem(me + step, blocks)
        pl.semaphore_signal(barrier, inc=1, device_id={"gx": other}, device_id_type=MESH)
    pl.semaphore_wait(barrier, blocks - 1)
    copies = []
    for step in range(1, blocks):
        copy = pltpu.make_async_remote_copy(
            src_ref=ends_ref,
            dst_ref=held_ref.at[step],
            send_sem=send_sems.at[step],
            recv_sem=recv_sems.at[step],
            device_id={"gx": lax.rem(me + step, blocks)},
            device_id_type=MESH,
        )
        copy.start()
        copies.append(copy)
    ratio = ratio_ref[...]

    def raised(base, count):
        value = None
        while count:
            if count & 1:
                value = base if value is None else value * base
            base = base * base
            count >>= 1
        return value

    across = raised(ratio, x_local)
    around = 1.0 / (1.0 - raised(across, blocks))
    both = ratio * ratio * (1.0 - across * across) / ((1.0 - ratio) * (1.0 + ratio))
    for copy in copies:
        copy.wait()

    def ends(step, which):
        return ends_ref[which] if step == 0 else held_ref[step, which]

    last = ends(blocks - 1, 0)
    for step in reversed(range(blocks - 1)):
        last = ends(step, 0) + across * last
    last = last * around
    tops = []
    for step in reversed(range(blocks)):
        enter_ref[...] = last
        tops.append(ends(step, 1) + both * last)
        last = ends(step, 0) + across * last
    first = tops[-1]
    for top in reversed(tops[:-1]):
        first = top + across * first
    leave_ref[...] = first * around


def link(ratio, own_ends, x_local, blocks):
    plane = jax.ShapeDtypeStruct(ratio.shape, f32)
    vmem = pl.BlockSpec(memory_space=pltpu.VMEM)
    return pl.pallas_call(
        functools.partial(link_kernel, x_local),
        out_shape=(plane, plane),
        in_specs=[vmem, vmem],
        out_specs=(vmem, vmem),
        scratch_shapes=[
            pltpu.VMEM((blocks,) + own_ends.shape, f32),
            pltpu.SemaphoreType.DMA((blocks,)),
            pltpu.SemaphoreType.DMA((blocks,)),
        ],
        compiler_params=pltpu.CompilerParams(
            collective_id=0, has_side_effects=True, vmem_limit_bytes=VMEM
        ),
        cost_estimate=cost(10 * blocks * own_ends.size, 4 * blocks * own_ends.size),
        name="link",
    )(ratio, own_ends)


def fall_kernel(
    first_row, value_ref, high_ref, low_ref, ratio_ref, enter_ref, leave_ref,
    out_ref, carry_ref, near_ref, far_ref, held_ref,
):
    layers, _, part = out_ref.shape
    ratio = ratio_ref[...]

    @pl.when(pl.program_id(0) == 0)
    def _():
        carry_ref[...] = leave_ref[...]
        power = ratio
        for x in range(ROWS):
            near_ref[x] = power
            if x < ROWS - 1:
                power = power * ratio
        value = enter_ref[...]
        for block in range(far_ref.shape[0]):
            far_ref[block] = value
            value = value * power

    step = pl.num_programs(0) - 1 - pl.program_id(0)
    value = carry_ref[...]
    for start in reversed(range(0, STEP, ROWS)):
        far = far_ref[(first_row + start) // ROWS + step * (STEP // ROWS)]
        for x in reversed(range(ROWS)):
            value = ratio * (value_ref[start + x] + near_ref[x] * far + value)
            held_ref[x * layers : (x + 1) * layers] = value
        solved = product((high_ref[...], low_ref[...]), split(held_ref[...]))
        out_ref[:, start : start + ROWS, :] = solved.reshape(layers, ROWS, part)
    carry_ref[...] = value


def fall(value, chunk, x_local, high, low, ratio, enter, leave):
    rows, layers, part = value.shape
    steps = rows // STEP
    table = pl.BlockSpec(high.shape, lambda i: (0, 0))
    plane = pl.BlockSpec((layers, part), lambda i: (0, 0))
    return pl.pallas_call(
        functools.partial(fall_kernel, chunk * rows),
        out_shape=(
            jax.ShapeDtypeStruct((layers, rows, part), f32),
            jax.ShapeDtypeStruct((layers, part), f32),
        ),
        grid=(steps,),
        in_specs=[
            pl.BlockSpec((STEP, layers, part), lambda i: (steps - 1 - i, 0, 0)),
            table, table, plane, plane, plane,
        ],
        out_specs=(
            pl.BlockSpec((layers, STEP, part), lambda i: (0, steps - 1 - i, 0)),
            plane,
        ),
        scratch_shapes=[
            pltpu.VMEM((ROWS, layers, part), f32),
            pltpu.VMEM((x_local // ROWS, layers, part), f32),
            pltpu.VMEM((ROWS * layers, part), f32),
        ],
        compiler_params=params(),
        cost_estimate=cost(6 * ROWS * layers * layers * rows * part, 8 * rows * layers * part),
        name="fall",
    )(value, high, low, ratio, enter, leave)


def back_y_kernel(value_ref, high_ref, low_ref, *rest):
    out_ref, rows_high, rows_low = rest[-3:]
    slabs, depth, rows, part = value_ref.shape

    @pl.when(pl.program_id(0) == 0)
    def _():
        for slab in range(slabs):
            high, low = split(value_ref[slab].reshape(depth * rows, part))
            rows_high[:, slab * part : (slab + 1) * part] = high
            rows_low[:, slab * part : (slab + 1) * part] = low

    result = product((rows_high[...], rows_low[...]), (high_ref[...], low_ref[...]))
    out_ref[...] = result.reshape(out_ref.shape)


def back_y(value, chunk, x_local, high, low, held):
    _, depth, rows, _ = value.shape
    width = high.shape[0]
    columns = min(256, width)
    operands = [value, high, low]
    in_specs = [
        pl.BlockSpec(value.shape, lambda i: (0, 0, 0, 0)),
        pl.BlockSpec((width, columns), lambda i: (0, i)),
        pl.BlockSpec((width, columns), lambda i: (0, i)),
    ]
    aliases = {}
    if held is not None:
        operands.append(held)
        in_specs.append(pl.BlockSpec(memory_space=pl.ANY))
        aliases = {3: 0}
    return pl.pallas_call(
        back_y_kernel,
        out_shape=jax.ShapeDtypeStruct((depth, x_local, width), f32),
        grid=(width // columns,),
        in_specs=in_specs,
        out_specs=pl.BlockSpec((depth, rows, columns), lambda i: (0, chunk, i)),
        scratch_shapes=[pltpu.VMEM((depth * rows, width), bf16)] * 2,
        input_output_aliases=aliases,
        compiler_params=params(),
        cost_estimate=cost(6 * depth * rows * width * width, 4 * width * width),
        name="back_y",
    )(*operands)


def body(charge, cell_permittivity, face_permittivity, screening):
    depth, x_local, width = charge.shape
    slabs = lax.axis_size("gz")
    layers = depth * slabs
    rows = x_local // CHUNKS
    part = width // slabs
    table = basis_table(width)
    fore_high, fore_low = halves(table * mode_weights(width)[None, :])
    back_high, back_low = halves(np.ascontiguousarray(table.T))
    shift_row = lax.dynamic_slice_in_dim(
        jnp.asarray(mode_shift(width)[None]), lax.axis_index("gz") * part, part, 1
    )
    exchange = functools.partial(
        lax.all_to_all, axis_name="gz", split_axis=0, concat_axis=0, tiled=True
    )
    layer_values = (cell_permittivity, face_permittivity, screening)
    sent = [forward_y(charge, 0, fore_high, fore_low, slabs, shift_row)]
    held = eigen_begin(*layer_values, sent[0])
    for chunk in range(1, CHUNKS):
        sent.append(forward_y(charge, chunk, fore_high, fore_low, slabs, held))
    ratio, to_high, to_low, from_high, from_low = eigen_end(
        held, *layer_values, shift_row, sent[-1]
    )
    state = None
    risen = []
    for chunk in range(CHUNKS):
        got = exchange(sent[chunk]).reshape(layers, rows, part)
        value, *state = rise(got, to_high, to_low, ratio, state)
        risen.append(value)
    enter, leave = link(ratio, state[0], x_local, lax.axis_size("gx"))
    result = None
    for chunk in reversed(range(CHUNKS)):
        sent, leave = fall(
            risen[chunk], chunk, x_local, from_high, from_low, ratio, enter, leave
        )
        got = exchange(sent.reshape(slabs, depth, rows, part))
        result = back_y(got, chunk, x_local, back_high, back_low, result)
    return result


def solution(mesh):
    in_specs = (P("gz", "gx", None), P(), P(), P())
    out_specs = P("gz", "gx", None)
    return jax.shard_map(body, mesh=mesh, in_specs=in_specs, out_specs=out_specs, check_vma=False)
```

```python
import functools

import jax
import jax.numpy as jnp
import ml_dtypes
import numpy as np
from jax import lax
from jax.experimental import pallas as pl
from jax.experimental.pallas import tpu as pltpu
from jax.sharding import PartitionSpec as P

f32 = jnp.float32
bf16 = jnp.bfloat16
LANES = 128
VMEM = 60 * 1024 * 1024
MESH = pl.DeviceIdType.MESH
ROWS = 8
CHUNKS = 4


def frequencies(length):
    col = np.arange(length)
    middle = length // 2
    return np.where(col <= middle, col, col - middle)


def basis_table(length):
    freq = frequencies(length)
    phase = (np.arange(length)[:, None] * freq[None, :]) % length
    angles = phase * (2.0 * np.pi / length)
    cos_part = np.arange(length)[None, :] <= length // 2
    return np.where(cos_part, np.cos(angles), np.sin(angles))


def halves(table):
    high = table.astype(ml_dtypes.bfloat16)
    low = (table - high.astype(np.float64)).astype(ml_dtypes.bfloat16)
    return jnp.asarray(high), jnp.asarray(low)


def mode_weights(length):
    col = np.arange(length)
    edge = (col == 0) | (col == length // 2)
    return np.where(edge, 1.0 / length, 2.0 / length)


def mode_shift(length):
    return (2.0 - 2.0 * np.cos(frequencies(length) * (2.0 * np.pi / length))).astype(np.float32)


def split(value):
    high = value.astype(bf16)
    low = (value - high.astype(f32)).astype(bf16)
    return high, low


def product(left, right):
    dot = functools.partial(jnp.dot, preferred_element_type=f32)
    return dot(left[0], right[0]) + (dot(left[0], right[1]) + dot(left[1], right[0]))


def one_stage(held, pair):
    n = held.shape[0]
    unit, mate, low_cols, low_rows, paired_cols, paired_rows = pair

    def lane_mates(value):
        return jnp.where(low_cols, pltpu.roll(value, LANES - 1, 1), pltpu.roll(value, 1, 1))

    def row_mates(value):
        return jnp.where(low_rows, pltpu.roll(value, n - 1, 0), pltpu.roll(value, 1, 0))

    def rotation(other, axis, low, paired):
        gap = jnp.sum(mate * other - unit * held, axis=axis, keepdims=True)
        twice = jnp.sum(mate * held + unit * other, axis=axis, keepdims=True)
        square = jnp.maximum(gap * gap + twice * twice, 1e-35)
        inverse = lax.rsqrt(square)
        inverse = inverse * (1.5 - 0.5 * square * inverse * inverse)
        inverse = inverse * (1.5 - 0.5 * square * inverse * inverse)
        half = 0.5 + 0.5 * jnp.abs(gap) * inverse
        root = lax.rsqrt(half)
        root = root * (1.5 - 0.5 * half * root * root)
        root = root * (1.5 - 0.5 * half * root * root)
        positive = (gap > 0.0) | ((gap == 0.0) & low)
        sine = 0.5 * jnp.where(positive, twice, -twice) * inverse * root
        return jnp.where(paired, sine, 1.0), jnp.where(paired, half * root, 0.0)

    by_lane = lane_mates(held)
    by_row = row_mates(held)
    by_both = row_mates(by_lane)
    own_row, cross_row = rotation(by_lane, 0, low_cols[:1], paired_cols[:1])
    own_col, cross_col = rotation(by_row, 1, low_rows[:, :1], paired_rows[:, :1])
    return own_col * (own_row * held + cross_row * by_lane) + cross_col * (
        own_row * by_row + cross_row * by_both
    )


def pairings(n):
    shape = (n, LANES)
    row = lax.broadcasted_iota(jnp.int32, shape, 0)
    col = lax.broadcasted_iota(jnp.int32, shape, 1)
    unit = (row == col).astype(f32)

    def pairing(parity):
        def lower(index):
            return ((index + parity) % 2 == 0) & (index < n - 1)

        def upper(index):
            return ((index + parity) % 2 == 1) & (index > 0) & (index < n)

        mate = jnp.where(lower(col), col + 1, jnp.where(upper(col), col - 1, -1))
        return (
            unit,
            (row == mate).astype(f32),
            lower(col),
            lower(row),
            lower(col) | upper(col),
            lower(row) | upper(row),
        )

    return pairing(0), pairing(1)


def one_sweep(held, pairs):
    def two(_, value):
        return one_stage(one_stage(value, pairs[0]), pairs[1])

    return lax.fori_loop(0, held.shape[0] // 2, two, held)


def eigenvectors(cell_col, cell_row, face_col, face_row, low_row, screen_row):
    n = cell_col.shape[0]
    row = lax.broadcasted_iota(jnp.int32, (n, LANES), 0)
    col = lax.broadcasted_iota(jnp.int32, (n, LANES), 1)
    tri = (
        (row == col).astype(f32) * (low_row + face_row + screen_row)
        - (col == row + 1).astype(f32) * face_col
        - (col == row - 1).astype(f32) * face_row
    )
    matrix = tri * (1.0 / jnp.sqrt(cell_col)) * (1.0 / jnp.sqrt(cell_row))
    held = jnp.where(col < n, matrix, (col == row + n).astype(f32))
    pairs = pairings(n)
    held = lax.fori_loop(0, n.bit_length(), lambda _, value: one_sweep(value, pairs), held)
    modes = jnp.where(col < n, pltpu.roll(held, LANES - n, 1), 0.0) / jnp.sqrt(cell_row)
    norm = jnp.sum(cell_row * modes * modes, axis=1, keepdims=True)
    modes = modes * (1.0 / jnp.sqrt(norm))
    slope = pltpu.roll(modes, LANES - 1, 1) - modes
    walls = jnp.where((col == 0) | (col == n - 1), 1.0, 0.0) * face_row[:, n - 1 : n]
    energy = (screen_row + walls) * modes * modes
    energy = energy + jnp.where(col < n - 1, face_row, 0.0) * slope * slope
    return modes, jnp.sum(energy, axis=1, keepdims=True)


def write_tables(modes, fores, backs):
    n = modes.shape[0]
    size = ROWS * n

    def flags(shape, test):
        first = lax.broadcasted_iota(jnp.int32, shape, 0)
        second = lax.broadcasted_iota(jnp.int32, shape, 1)
        return jnp.where(test(first, second), 1.0, 0.0)

    pick_mode = flags((size, n), lambda a, b: a % n == b).astype(bf16)
    spread_mode = flags((n, size), lambda a, b: b % n == a).astype(bf16)
    pick_layer = flags((size, LANES), lambda a, b: a // ROWS == b).astype(bf16)
    spread_layer = flags((LANES, size), lambda a, b: b // ROWS == a).astype(bf16)
    same_fore = flags((size, size), lambda a, b: a // n == b % ROWS)
    same_back = flags((size, size), lambda a, b: a % ROWS == b // n)
    across = (((1,), (1,)), ((), ()))
    for part, fore, back in zip(split(modes), fores, backs):
        turned = jnp.dot(pick_mode, part, preferred_element_type=f32)
        spread = jnp.dot(turned.astype(bf16), spread_layer, preferred_element_type=f32)
        fore[...] = (spread * same_fore).astype(bf16)
        layered = lax.dot_general(pick_layer, part, across, preferred_element_type=f32)
        spread = jnp.dot(layered.astype(bf16), spread_mode, preferred_element_type=f32)
        back[...] = (spread * same_back).astype(bf16)


def raised(base, count):
    value = None
    while count:
        if count & 1:
            value = base if value is None else value * base
        base = base * base
        count >>= 1
    return value


def entering_values(ratio, x_local, blocks, ends):
    across = raised(ratio, x_local)
    around = 1.0 / (1.0 - raised(across, blocks))
    both = ratio * ratio * (1.0 - across * across) / ((1.0 - ratio) * (1.0 + ratio))
    last = ends(blocks - 1, 0)
    for step in reversed(range(blocks - 1)):
        last = ends(step, 0) + across * last
    last = last * around
    tops = []
    enter = last
    for step in reversed(range(blocks)):
        enter = last
        tops.append(ends(step, 1) + both * last)
        last = ends(step, 0) + across * last
    first = tops[-1]
    for top in reversed(tops[:-1]):
        first = top + across * first
    return enter, first * around


def kernel(
    charge, fore_high, fore_low, back_high_in, back_low_in,
    cell_col, cell_row, face_col, face_row, low_row, screen_row, shift_row,
    out,
    sent, got, risen, returned, arrived, result, back_high, back_low,
    to_high, to_low, from_high, from_low, ratio_ref, near, far, turn, ends, linked, flow,
    send_sems, recv_sems, return_sems, arrive_sems, link_send, link_recv, table_sems, out_sems,
):
    depth, x_local, width = charge.shape
    slabs, blocks = sent.shape[1], linked.shape[0]
    layers, part = ratio_ref.shape
    rows = x_local // CHUNKS
    tiles = rows // ROWS
    me, place = lax.axis_index("gz"), lax.axis_index("gx")

    tables = [
        pltpu.make_async_copy(back_high_in, back_high, table_sems.at[0]),
        pltpu.make_async_copy(back_low_in, back_low, table_sems.at[1]),
    ]
    for table in tables:
        table.start()
    barrier = pltpu.get_barrier_semaphore()
    for axis, own, count in (("gz", me, slabs), ("gx", place, blocks)):
        for step in range(1, count):
            other = lax.rem(own + step, count)
            pl.semaphore_signal(barrier, inc=1, device_id={axis: other}, device_id_type=MESH)
    pl.semaphore_wait(barrier, slabs + blocks - 2)

    def send(chunk, step):
        other = lax.rem(me + step, slabs)
        return pltpu.make_async_remote_copy(
            src_ref=sent.at[chunk, step],
            dst_ref=got.at[chunk, step],
            send_sem=send_sems.at[chunk, step],
            recv_sem=recv_sems.at[chunk, step],
            device_id={"gz": other},
            device_id_type=MESH,
        )

    def forward_y(chunk, _):
        start = pl.multiple_of(chunk * rows, rows)
        left = split(charge[:, pl.ds(start, rows), :].reshape(depth * rows, width))
        for step in list(range(1, slabs)) + [0]:
            other = lax.rem(me + step, slabs)
            value = product(left, (fore_high[other], fore_low[other]))
            value = value.reshape(depth, rows, part)
            if step:
                sent[chunk, step] = value
                send(chunk, step).start()
            else:
                got[chunk, 0] = value
        return 0

    lax.fori_loop(0, CHUNKS, forward_y, 0)

    modes, values = eigenvectors(
        cell_col[...], cell_row[...], face_col[...], face_row[...], low_row[...], screen_row[...]
    )
    write_tables(modes, (to_high, to_low), (from_high, from_low))
    total = values + shift_row[...]
    ratio = 2.0 / (2.0 + total + jnp.sqrt(total * (total + 4.0)))
    ratio_ref[...] = ratio

    ends[...] = jnp.zeros_like(ends)
    flow[...] = ratio

    def rise(chunk, _):
        for step in range(1, slabs):
            send(chunk, step).wait_recv()

        def tile(index, _):
            start = pl.multiple_of(index * ROWS, ROWS)
            parts = [
                got[chunk, lax.rem(me + (slabs - slab), slabs), :, pl.ds(start, ROWS), :]
                for slab in range(slabs)
            ]
            block = jnp.concatenate(parts, axis=0).reshape(layers * ROWS, part)
            turn[...] = product((to_high[...], to_low[...]), split(block))
            ratio = ratio_ref[...]
            value, total, power = ends[0], ends[1], flow[...]
            for x in range(ROWS):
                value = turn[x * layers : (x + 1) * layers] + ratio * value
                risen[chunk * rows + start + x] = value
                total = total + power * value
                power = power * ratio
            ends[0] = value
            ends[1] = total
            flow[...] = power
            return 0

        lax.fori_loop(0, tiles, tile, 0)
        return 0

    lax.fori_loop(0, CHUNKS, rise, 0)

    links = []
    for step in range(1, blocks):
        copy = pltpu.make_async_remote_copy(
            src_ref=ends,
            dst_ref=linked.at[step],
            send_sem=link_send.at[step],
            recv_sem=link_recv.at[step],
            device_id={"gx": lax.rem(place + step, blocks)},
            device_id_type=MESH,
        )
        copy.start()
        links.append(copy)
    power = ratio_ref[...]
    for x in range(ROWS):
        near[x] = power
        if x < ROWS - 1:
            power = power * ratio_ref[...]
    for copy in links:
        copy.wait()
    enter, leave = entering_values(
        ratio_ref[...], x_local, blocks,
        lambda step, which: linked[step, which] if step else ends[which],
    )
    flow[...] = leave
    power = near[ROWS - 1]
    for block in range(x_local // ROWS):
        far[block] = enter
        enter = enter * power

    def give_back(chunk, step):
        other = lax.rem(me + step, slabs)
        return pltpu.make_async_remote_copy(
            src_ref=returned.at[chunk, other],
            dst_ref=arrived.at[chunk, step],
            send_sem=return_sems.at[chunk, step],
            recv_sem=arrive_sems.at[chunk, step],
            device_id={"gz": other},
            device_id_type=MESH,
        )

    def fall(turned, _):
        chunk = CHUNKS - 1 - turned

        def tile(turned, _):
            index = tiles - 1 - turned
            start = pl.multiple_of(index * ROWS, ROWS)
            ratio = ratio_ref[...]
            value = flow[...]
            entered = far[chunk * tiles + index]
            for x in reversed(range(ROWS)):
                value = ratio * (risen[chunk * rows + start + x] + near[x] * entered + value)
                turn[x * layers : (x + 1) * layers] = value
            flow[...] = value
            solved = product((from_high[...], from_low[...]), split(turn[...]))
            returned[chunk, :, :, pl.ds(start, ROWS), :] = solved.reshape(
                slabs, depth, ROWS, part
            )
            return 0

        lax.fori_loop(0, tiles, tile, 0)
        for step in range(1, slabs):
            give_back(chunk, step).start()
        return 0

    lax.fori_loop(0, CHUNKS, fall, 0)
    for table in tables:
        table.wait()

    def write(chunk):
        place = pl.ds(pl.multiple_of(chunk * rows, rows), rows)
        return pltpu.make_async_copy(
            result.at[chunk], out.at[:, place, :], out_sems.at[chunk]
        )

    def back_y(turned, _):
        chunk = CHUNKS - 1 - turned
        total = None
        for step in range(slabs):
            if step:
                give_back(chunk, step).wait_recv()
                value = arrived[chunk, step]
            else:
                value = returned[chunk, me]
            source = lax.rem(me + (slabs - step), slabs)
            left = split(value.reshape(depth * rows, part))
            term = product(left, (back_high[source], back_low[source]))
            total = term if total is None else total + term
        result[chunk] = total.reshape(depth, rows, width)
        write(chunk).start()
        return 0

    lax.fori_loop(0, CHUNKS, back_y, 0)

    def settle(chunk, _):
        for step in range(1, slabs):
            send(chunk, step).wait_send()
            give_back(chunk, step).wait_send()
        write(chunk).wait()
        return 0

    lax.fori_loop(0, CHUNKS, settle, 0)


def as_row(value):
    return jnp.pad(value, (0, LANES - value.shape[0]), constant_values=1.0)[None]


def body(charge, cell, face, screening):
    depth, x_local, width = charge.shape
    slabs, blocks = lax.axis_size("gz"), lax.axis_size("gx")
    layers, part, rows = depth * slabs, width // slabs, x_local // CHUNKS
    table = basis_table(width)
    fore = (table * mode_weights(width)[None, :]).reshape(width, slabs, part).transpose(1, 0, 2)
    back = table.T.reshape(slabs, part, width)
    shift_row = lax.dynamic_slice_in_dim(
        jnp.asarray(mode_shift(width)[None]), lax.axis_index("gz") * part, part, 1
    )
    vmem, anywhere = pl.BlockSpec(memory_space=pltpu.VMEM), pl.BlockSpec(memory_space=pl.ANY)
    chunked = pltpu.VMEM((CHUNKS, slabs, depth, rows, part), f32)
    square = pltpu.VMEM((ROWS * layers, ROWS * layers), bf16)
    plane = pltpu.VMEM((layers, part), f32)
    many = pltpu.SemaphoreType.DMA((CHUNKS, slabs))
    return pl.pallas_call(
        kernel,
        out_shape=jax.ShapeDtypeStruct(charge.shape, f32),
        in_specs=[vmem, vmem, vmem, anywhere, anywhere] + [vmem] * 7,
        out_specs=anywhere,
        scratch_shapes=[
            chunked,
            chunked,
            pltpu.VMEM((x_local, layers, part), f32),
            chunked,
            chunked,
            pltpu.VMEM((CHUNKS, depth, rows, width), f32),
            pltpu.VMEM((slabs, part, width), bf16),
            pltpu.VMEM((slabs, part, width), bf16),
            square,
            square,
            square,
            square,
            plane,
            pltpu.VMEM((ROWS, layers, part), f32),
            pltpu.VMEM((x_local // ROWS, layers, part), f32),
            pltpu.VMEM((ROWS * layers, part), f32),
            pltpu.VMEM((2, layers, part), f32),
            pltpu.VMEM((blocks, 2, layers, part), f32),
            plane,
            many,
            many,
            many,
            many,
            pltpu.SemaphoreType.DMA((blocks,)),
            pltpu.SemaphoreType.DMA((blocks,)),
            pltpu.SemaphoreType.DMA((2,)),
            pltpu.SemaphoreType.DMA((CHUNKS,)),
        ],
        compiler_params=pltpu.CompilerParams(
            collective_id=0, has_side_effects=True, vmem_limit_bytes=VMEM
        ),
        cost_estimate=pl.CostEstimate(
            flops=12 * depth * x_local * width * width,
            bytes_accessed=8 * charge.size,
            transcendentals=0,
        ),
        name="precondition",
    )(
        charge, *halves(fore), *halves(back),
        cell[:, None], as_row(cell), face[:, None], as_row(face), as_row(jnp.roll(face, 1)),
        as_row(screening), shift_row,
    )


def solution(mesh):
    in_specs = (P("gz", "gx", None), P(), P(), P())
    out_specs = P("gz", "gx", None)
    return jax.shard_map(body, mesh=mesh, in_specs=in_specs, out_specs=out_specs, check_vma=False)
```

```python
import functools

import jax
import jax.numpy as jnp
import ml_dtypes
import numpy as np
from jax import lax
from jax.experimental import pallas as pl
from jax.experimental.pallas import tpu as pltpu
from jax.sharding import PartitionSpec as P

f32 = jnp.float32
bf16 = jnp.bfloat16
LANES = 128
VMEM = 60 * 1024 * 1024
MESH = pl.DeviceIdType.MESH
ROWS = 8
HALF = 128
CHUNKS = 4


def frequencies(length):
    col = np.arange(length)
    middle = length // 2
    return np.where(col <= middle, col, col - middle)


def basis_table(length):
    freq = frequencies(length)
    phase = (np.arange(length)[:, None] * freq[None, :]) % length
    angles = phase * (2.0 * np.pi / length)
    cos_part = np.arange(length)[None, :] <= length // 2
    return np.where(cos_part, np.cos(angles), np.sin(angles))


def halves(table):
    high = table.astype(ml_dtypes.bfloat16)
    low = (table - high.astype(np.float64)).astype(ml_dtypes.bfloat16)
    return jnp.asarray(high), jnp.asarray(low)


def mode_weights(length):
    col = np.arange(length)
    edge = (col == 0) | (col == length // 2)
    return np.where(edge, 1.0 / length, 2.0 / length)


def mode_shift(length):
    return (2.0 - 2.0 * np.cos(frequencies(length) * (2.0 * np.pi / length))).astype(np.float32)


def split(value):
    high = value.astype(bf16)
    low = (value - high.astype(f32)).astype(bf16)
    return high, low


def product(left, right):
    dot = functools.partial(jnp.dot, preferred_element_type=f32)
    return dot(left[0], right[0]) + (dot(left[0], right[1]) + dot(left[1], right[0]))


def one_stage(held, pair):
    n = held.shape[0]
    unit, mate, low_cols, low_rows, paired_cols, paired_rows = pair

    def lane_mates(value):
        return jnp.where(low_cols, pltpu.roll(value, LANES - 1, 1), pltpu.roll(value, 1, 1))

    def row_mates(value):
        return jnp.where(low_rows, pltpu.roll(value, n - 1, 0), pltpu.roll(value, 1, 0))

    def rotation(other, axis, low, paired):
        gap = jnp.sum(mate * other - unit * held, axis=axis, keepdims=True)
        twice = jnp.sum(mate * held + unit * other, axis=axis, keepdims=True)
        square = jnp.maximum(gap * gap + twice * twice, 1e-35)
        inverse = lax.rsqrt(square)
        inverse = inverse * (1.5 - 0.5 * square * inverse * inverse)
        inverse = inverse * (1.5 - 0.5 * square * inverse * inverse)
        half = 0.5 + 0.5 * jnp.abs(gap) * inverse
        root = lax.rsqrt(half)
        root = root * (1.5 - 0.5 * half * root * root)
        root = root * (1.5 - 0.5 * half * root * root)
        positive = (gap > 0.0) | ((gap == 0.0) & low)
        sine = 0.5 * jnp.where(positive, twice, -twice) * inverse * root
        return jnp.where(paired, sine, 1.0), jnp.where(paired, half * root, 0.0)

    by_lane = lane_mates(held)
    by_row = row_mates(held)
    by_both = row_mates(by_lane)
    own_row, cross_row = rotation(by_lane, 0, low_cols[:1], paired_cols[:1])
    own_col, cross_col = rotation(by_row, 1, low_rows[:, :1], paired_rows[:, :1])
    return own_col * (own_row * held + cross_row * by_lane) + cross_col * (
        own_row * by_row + cross_row * by_both
    )


def pairings(n):
    shape = (n, LANES)
    row = lax.broadcasted_iota(jnp.int32, shape, 0)
    col = lax.broadcasted_iota(jnp.int32, shape, 1)
    unit = (row == col).astype(f32)

    def pairing(parity):
        def lower(index):
            return ((index + parity) % 2 == 0) & (index < n - 1)

        def upper(index):
            return ((index + parity) % 2 == 1) & (index > 0) & (index < n)

        mate = jnp.where(lower(col), col + 1, jnp.where(upper(col), col - 1, -1))
        return (
            unit,
            (row == mate).astype(f32),
            lower(col),
            lower(row),
            lower(col) | upper(col),
            lower(row) | upper(row),
        )

    return pairing(0), pairing(1)


def eigen_start(cell_col, cell_row, face_col, face_row, low_row, screen_row):
    n = cell_col.shape[0]
    row = lax.broadcasted_iota(jnp.int32, (n, LANES), 0)
    col = lax.broadcasted_iota(jnp.int32, (n, LANES), 1)
    tri = (
        (row == col).astype(f32) * (low_row + face_row + screen_row)
        - (col == row + 1).astype(f32) * face_col
        - (col == row - 1).astype(f32) * face_row
    )
    matrix = tri * (1.0 / jnp.sqrt(cell_col)) * (1.0 / jnp.sqrt(cell_row))
    return jnp.where(col < n, matrix, (col == row + n).astype(f32))


def eigen_finish(held, cell_row, face_row, screen_row):
    n = held.shape[0]
    col = lax.broadcasted_iota(jnp.int32, (n, LANES), 1)
    modes = jnp.where(col < n, pltpu.roll(held, LANES - n, 1), 0.0) / jnp.sqrt(cell_row)
    norm = jnp.sum(cell_row * modes * modes, axis=1, keepdims=True)
    modes = modes * (1.0 / jnp.sqrt(norm))
    slope = pltpu.roll(modes, LANES - 1, 1) - modes
    walls = jnp.where((col == 0) | (col == n - 1), 1.0, 0.0) * face_row[:, n - 1 : n]
    energy = (screen_row + walls) * modes * modes
    energy = energy + jnp.where(col < n - 1, face_row, 0.0) * slope * slope
    return modes, jnp.sum(energy, axis=1, keepdims=True)


def write_tables(modes, fores, backs):
    n = modes.shape[0]
    size = ROWS * n

    def flags(shape, test):
        first = lax.broadcasted_iota(jnp.int32, shape, 0)
        second = lax.broadcasted_iota(jnp.int32, shape, 1)
        return jnp.where(test(first, second), 1.0, 0.0)

    pick_mode = flags((size, n), lambda a, b: a % n == b).astype(bf16)
    spread_mode = flags((n, size), lambda a, b: b % n == a).astype(bf16)
    pick_layer = flags((size, LANES), lambda a, b: a // ROWS == b).astype(bf16)
    spread_layer = flags((LANES, size), lambda a, b: b // ROWS == a).astype(bf16)
    same_fore = flags((size, size), lambda a, b: a // n == b % ROWS)
    same_back = flags((size, size), lambda a, b: a % ROWS == b // n)
    across = (((1,), (1,)), ((), ()))
    for part, fore, back in zip(split(modes), fores, backs):
        turned = jnp.dot(pick_mode, part, preferred_element_type=f32)
        spread = jnp.dot(turned.astype(bf16), spread_layer, preferred_element_type=f32)
        fore[...] = (spread * same_fore).astype(bf16)
        layered = lax.dot_general(pick_layer, part, across, preferred_element_type=f32)
        spread = jnp.dot(layered.astype(bf16), spread_mode, preferred_element_type=f32)
        back[...] = (spread * same_back).astype(bf16)


def raised(base, count):
    value = None
    while count:
        if count & 1:
            value = base if value is None else value * base
        base = base * base
        count >>= 1
    return value


def entering_values(ratio, x_local, blocks, ends):
    across = raised(ratio, x_local)
    around = 1.0 / (1.0 - raised(across, blocks))
    both = ratio * ratio * (1.0 - across * across) / ((1.0 - ratio) * (1.0 + ratio))
    last = ends(blocks - 1, 0)
    for step in reversed(range(blocks - 1)):
        last = ends(step, 0) + across * last
    last = last * around
    tops = []
    enter = last
    for step in reversed(range(blocks)):
        enter = last
        tops.append(ends(step, 1) + both * last)
        last = ends(step, 0) + across * last
    first = tops[-1]
    for top in reversed(tops[:-1]):
        first = top + across * first
    return enter, first * around


def kernel(
    charge, fore_high, fore_low, back_high_in, back_low_in, cell, face, screening, shift,
    out,
    plain, sent, got, risen, returned, arrived, result, back_high, back_low,
    to_high, to_low, from_high, from_low, ratio_ref, near, far, turn, ends, linked, flow,
    send_sems, recv_sems, return_sems, arrive_sems, link_send, link_recv, table_sems, out_sems,
):
    depth, x_local, width = charge.shape
    slabs = sent.shape[1]
    halves_of, layers, half_part = ratio_ref.shape
    blocks = linked.shape[1]
    part = halves_of * half_part
    rows = x_local // CHUNKS
    tiles = rows // ROWS
    me, place = lax.axis_index("gz"), lax.axis_index("gx")

    tables = [
        pltpu.make_async_copy(back_high_in, back_high, table_sems.at[0]),
        pltpu.make_async_copy(back_low_in, back_low, table_sems.at[1]),
    ]
    for table in tables:
        table.start()
    barrier = pltpu.get_barrier_semaphore()
    for axis, own, count in (("gz", me, slabs), ("gx", place, blocks)):
        for step in range(1, count):
            other = lax.rem(own + step, count)
            pl.semaphore_signal(barrier, inc=1, device_id={axis: other}, device_id_type=MESH)

    plain[...] = jnp.ones_like(plain)
    for index, value in enumerate((cell, face, screening)):
        plain[index : index + 1, 0:layers] = value[...]
    cell_row, face_row, screen_row = plain[0:1], plain[1:2], plain[2:3]
    unit = lax.broadcasted_iota(jnp.int32, (layers, LANES), 0) == lax.broadcasted_iota(
        jnp.int32, (layers, LANES), 1
    )
    cell_col = jnp.sum(jnp.where(unit, cell_row, 0.0), axis=1, keepdims=True)
    face_col = jnp.sum(jnp.where(unit, face_row, 0.0), axis=1, keepdims=True)
    lane = lax.broadcasted_iota(jnp.int32, (1, LANES), 1)
    low_row = jnp.where(lane == 0, face_row[:, layers - 1 : layers], pltpu.roll(face_row, 1, 1))
    held = eigen_start(cell_col, cell_row, face_col, face_row, low_row, screen_row)
    pairs = pairings(layers)
    turns = -(-layers.bit_length() * (layers // 2) // (CHUNKS * slabs))
    pl.semaphore_wait(barrier, slabs + blocks - 2)

    def send(half, chunk, step):
        slot = half * CHUNKS + chunk
        return pltpu.make_async_remote_copy(
            src_ref=sent.at[slot, step],
            dst_ref=got.at[slot, step],
            send_sem=send_sems.at[slot, step],
            recv_sem=recv_sems.at[slot, step],
            device_id={"gz": lax.rem(me + step, slabs)},
            device_id_type=MESH,
        )

    def forward_y(chunk, held):
        start = pl.multiple_of(chunk * rows, rows)
        left = split(charge[:, pl.ds(start, rows), :].reshape(depth * rows, width))
        for step in list(range(1, slabs)) + [0]:
            other = lax.rem(me + step, slabs)
            value = product(left, (fore_high[other], fore_low[other]))
            for _ in range(turns):
                held = one_stage(one_stage(held, pairs[0]), pairs[1])
            value = value.reshape(depth, rows, part)
            for half in range(halves_of):
                piece = value[:, :, half * half_part : (half + 1) * half_part]
                if step:
                    sent[half * CHUNKS + chunk, step] = piece
                else:
                    got[half * CHUNKS + chunk, 0] = piece
            if step:
                send(0, chunk, step).start()
        return held

    held = lax.fori_loop(0, CHUNKS, forward_y, held)

    def send_rest(chunk, _):
        for half in range(1, halves_of):
            for step in range(1, slabs):
                send(half, chunk, step).start()
        return 0

    lax.fori_loop(0, CHUNKS, send_rest, 0)

    modes, values = eigen_finish(held, cell_row, face_row, screen_row)
    write_tables(modes, (to_high, to_low), (from_high, from_low))
    total = values + shift[me]
    ratio = 2.0 / (2.0 + total + jnp.sqrt(total * (total + 4.0)))
    for half in range(halves_of):
        ratio_ref[half] = ratio[:, half * half_part : (half + 1) * half_part]

    def give_back(half, chunk, step):
        slot = half * CHUNKS + chunk
        other = lax.rem(me + step, slabs)
        return pltpu.make_async_remote_copy(
            src_ref=returned.at[slot, other],
            dst_ref=arrived.at[slot, step],
            send_sem=return_sems.at[slot, step],
            recv_sem=arrive_sems.at[slot, step],
            device_id={"gz": other},
            device_id_type=MESH,
        )

    def solve(half):
        ends[half] = jnp.zeros(ends.shape[1:], f32)
        flow[...] = ratio_ref[half]

        def rise(chunk, _):
            for step in range(1, slabs):
                send(half, chunk, step).wait_recv()

            def tile(index, _):
                start = pl.multiple_of(index * ROWS, ROWS)
                slot = half * CHUNKS + chunk
                parts = [
                    got[slot, lax.rem(me + (slabs - slab), slabs), :, pl.ds(start, ROWS), :]
                    for slab in range(slabs)
                ]
                block = jnp.concatenate(parts, axis=0).reshape(layers * ROWS, half_part)
                turn[...] = product((to_high[...], to_low[...]), split(block))
                ratio = ratio_ref[half]
                value, total, power = ends[half, 0], ends[half, 1], flow[...]
                for x in range(ROWS):
                    value = turn[x * layers : (x + 1) * layers] + ratio * value
                    risen[chunk * rows + start + x] = value
                    total = total + power * value
                    power = power * ratio
                ends[half, 0] = value
                ends[half, 1] = total
                flow[...] = power
                return 0

            lax.fori_loop(0, tiles, tile, 0)
            return 0

        lax.fori_loop(0, CHUNKS, rise, 0)

        links = []
        for step in range(1, blocks):
            copy = pltpu.make_async_remote_copy(
                src_ref=ends.at[half],
                dst_ref=linked.at[half, step],
                send_sem=link_send.at[half, step],
                recv_sem=link_recv.at[half, step],
                device_id={"gx": lax.rem(place + step, blocks)},
                device_id_type=MESH,
            )
            copy.start()
            links.append(copy)
        power = ratio_ref[half]
        for x in range(ROWS):
            near[x] = power
            if x < ROWS - 1:
                power = power * ratio_ref[half]
        for copy in links:
            copy.wait()
        enter, leave = entering_values(
            ratio_ref[half], x_local, blocks,
            lambda step, which: linked[half, step, which] if step else ends[half, which],
        )
        flow[...] = leave
        power = near[ROWS - 1]
        for block in range(x_local // ROWS):
            far[block] = enter
            enter = enter * power

        def fall(turned, _):
            chunk = CHUNKS - 1 - turned

            def tile(turned, _):
                index = tiles - 1 - turned
                start = pl.multiple_of(index * ROWS, ROWS)
                ratio = ratio_ref[half]
                value = flow[...]
                entered = far[chunk * tiles + index]
                for x in reversed(range(ROWS)):
                    value = ratio * (risen[chunk * rows + start + x] + near[x] * entered + value)
                    turn[x * layers : (x + 1) * layers] = value
                flow[...] = value
                solved = product((from_high[...], from_low[...]), split(turn[...]))
                returned[half * CHUNKS + chunk, :, :, pl.ds(start, ROWS), :] = solved.reshape(
                    slabs, depth, ROWS, half_part
                )
                return 0

            lax.fori_loop(0, tiles, tile, 0)
            for step in range(1, slabs):
                give_back(half, chunk, step).start()
            return 0

        lax.fori_loop(0, CHUNKS, fall, 0)

    for half in range(halves_of):
        solve(half)
    for table in tables:
        table.wait()

    def write(chunk):
        place = pl.ds(pl.multiple_of(chunk * rows, rows), rows)
        return pltpu.make_async_copy(
            result.at[chunk], out.at[:, place, :], out_sems.at[chunk]
        )

    def back_y(turned, _):
        chunk = CHUNKS - 1 - turned
        total = None
        for step in range(slabs):
            pieces = []
            for half in range(halves_of):
                slot = half * CHUNKS + chunk
                if step:
                    give_back(half, chunk, step).wait_recv()
                    value = arrived[slot, step]
                else:
                    value = returned[slot, me]
                pieces.append(value.reshape(depth * rows, half_part))
            source = lax.rem(me + (slabs - step), slabs)
            left = split(pieces[0] if halves_of == 1 else jnp.concatenate(pieces, axis=1))
            term = product(left, (back_high[source], back_low[source]))
            total = term if total is None else total + term
        result[chunk] = total.reshape(depth, rows, width)
        write(chunk).start()
        return 0

    lax.fori_loop(0, CHUNKS, back_y, 0)

    def settle(chunk, _):
        for half in range(halves_of):
            for step in range(1, slabs):
                send(half, chunk, step).wait_send()
                give_back(half, chunk, step).wait_send()
        write(chunk).wait()
        return 0

    lax.fori_loop(0, CHUNKS, settle, 0)


def body(charge, cell, face, screening):
    depth, x_local, width = charge.shape
    slabs, blocks = lax.axis_size("gz"), lax.axis_size("gx")
    layers, part, rows = depth * slabs, width // slabs, x_local // CHUNKS
    half_part = HALF if part % HALF == 0 else part
    halves_of = part // half_part
    table = basis_table(width)
    fore = (table * mode_weights(width)[None, :]).reshape(width, slabs, part).transpose(1, 0, 2)
    back = table.T.reshape(slabs, part, width)
    shift = jnp.asarray(mode_shift(width).reshape(slabs, 1, part))
    vmem, anywhere = pl.BlockSpec(memory_space=pltpu.VMEM), pl.BlockSpec(memory_space=pl.ANY)
    slots = halves_of * CHUNKS
    chunked = pltpu.VMEM((slots, slabs, depth, rows, half_part), f32)
    square = pltpu.VMEM((ROWS * layers, ROWS * layers), bf16)
    many = pltpu.SemaphoreType.DMA((slots, slabs))
    return pl.pallas_call(
        kernel,
        out_shape=jax.ShapeDtypeStruct(charge.shape, f32),
        in_specs=[vmem, vmem, vmem, anywhere, anywhere] + [vmem] * 4,
        out_specs=anywhere,
        scratch_shapes=[
            pltpu.VMEM((8, LANES), f32),
            chunked,
            chunked,
            pltpu.VMEM((x_local, layers, half_part), f32),
            chunked,
            chunked,
            pltpu.VMEM((CHUNKS, depth, rows, width), f32),
            pltpu.VMEM((slabs, part, width), bf16),
            pltpu.VMEM((slabs, part, width), bf16),
            square,
            square,
            square,
            square,
            pltpu.VMEM((halves_of, layers, half_part), f32),
            pltpu.VMEM((ROWS, layers, half_part), f32),
            pltpu.VMEM((x_local // ROWS, layers, half_part), f32),
            pltpu.VMEM((ROWS * layers, half_part), f32),
            pltpu.VMEM((halves_of, 2, layers, half_part), f32),
            pltpu.VMEM((halves_of, blocks, 2, layers, half_part), f32),
            pltpu.VMEM((layers, half_part), f32),
            many,
            many,
            many,
            many,
            pltpu.SemaphoreType.DMA((halves_of, blocks)),
            pltpu.SemaphoreType.DMA((halves_of, blocks)),
            pltpu.SemaphoreType.DMA((2,)),
            pltpu.SemaphoreType.DMA((CHUNKS,)),
        ],
        compiler_params=pltpu.CompilerParams(
            collective_id=0, has_side_effects=True, vmem_limit_bytes=VMEM
        ),
        cost_estimate=pl.CostEstimate(
            flops=12 * depth * x_local * width * width,
            bytes_accessed=8 * charge.size,
            transcendentals=0,
        ),
        name="precondition",
    )(
        charge, *halves(fore), *halves(back), cell[None], face[None], screening[None], shift
    )


def solution(mesh):
    in_specs = (P("gz", "gx", None), P(), P(), P())
    out_specs = P("gz", "gx", None)
    return jax.shard_map(body, mesh=mesh, in_specs=in_specs, out_specs=out_specs, check_vma=False)
```

```python
import functools

import jax
import jax.numpy as jnp
import ml_dtypes
import numpy as np
from jax import lax
from jax.experimental import pallas as pl
from jax.experimental.pallas import tpu as pltpu
from jax.sharding import PartitionSpec as P

f32 = jnp.float32
bf16 = jnp.bfloat16
LANES = 128
VMEM = 60 * 1024 * 1024
MESH = pl.DeviceIdType.MESH
ROWS = 8
HALF = 128
CHUNKS = 4


def frequencies(length):
    col = np.arange(length)
    middle = length // 2
    return np.where(col <= middle, col, col - middle)


def basis_table(length):
    freq = frequencies(length)
    phase = (np.arange(length)[:, None] * freq[None, :]) % length
    angles = phase * (2.0 * np.pi / length)
    cos_part = np.arange(length)[None, :] <= length // 2
    return np.where(cos_part, np.cos(angles), np.sin(angles))


def halves(table):
    high = table.astype(ml_dtypes.bfloat16)
    low = (table - high.astype(np.float64)).astype(ml_dtypes.bfloat16)
    return jnp.asarray(high), jnp.asarray(low)


def mode_weights(length):
    col = np.arange(length)
    edge = (col == 0) | (col == length // 2)
    return np.where(edge, 1.0 / length, 2.0 / length)


def mode_shift(length):
    return (2.0 - 2.0 * np.cos(frequencies(length) * (2.0 * np.pi / length))).astype(np.float32)


def split(value):
    high = value.astype(bf16)
    low = (value - high.astype(f32)).astype(bf16)
    return high, low


def product(left, right):
    dot = functools.partial(jnp.dot, preferred_element_type=f32)
    return dot(left[0], right[0]) + (dot(left[0], right[1]) + dot(left[1], right[0]))


def one_stage(held, pair):
    n = held.shape[0]
    unit, mate, low_cols, low_rows, paired_cols, paired_rows = pair

    def lane_mates(value):
        return jnp.where(low_cols, pltpu.roll(value, LANES - 1, 1), pltpu.roll(value, 1, 1))

    def row_mates(value):
        return jnp.where(low_rows, pltpu.roll(value, n - 1, 0), pltpu.roll(value, 1, 0))

    def rotation(other, axis, low, paired):
        gap = jnp.sum(mate * other - unit * held, axis=axis, keepdims=True)
        twice = jnp.sum(mate * held + unit * other, axis=axis, keepdims=True)
        square = jnp.maximum(gap * gap + twice * twice, 1e-35)
        inverse = lax.rsqrt(square)
        inverse = inverse * (1.5 - 0.5 * square * inverse * inverse)
        half = 0.5 + 0.5 * jnp.abs(gap) * inverse
        root = lax.rsqrt(half)
        root = root * (1.5 - 0.5 * half * root * root)
        positive = (gap > 0.0) | ((gap == 0.0) & low)
        sine = 0.5 * jnp.where(positive, twice, -twice) * inverse * root
        return jnp.where(paired, sine, 1.0), jnp.where(paired, half * root, 0.0)

    by_lane = lane_mates(held)
    by_row = row_mates(held)
    by_both = row_mates(by_lane)
    own_row, cross_row = rotation(by_lane, 0, low_cols[:1], paired_cols[:1])
    own_col, cross_col = rotation(by_row, 1, low_rows[:, :1], paired_rows[:, :1])
    return own_col * (own_row * held + cross_row * by_lane) + cross_col * (
        own_row * by_row + cross_row * by_both
    )


def pairings(n):
    shape = (n, LANES)
    row = lax.broadcasted_iota(jnp.int32, shape, 0)
    col = lax.broadcasted_iota(jnp.int32, shape, 1)
    unit = (row == col).astype(f32)

    def pairing(parity):
        def lower(index):
            return ((index + parity) % 2 == 0) & (index < n - 1)

        def upper(index):
            return ((index + parity) % 2 == 1) & (index > 0) & (index < n)

        mate = jnp.where(lower(col), col + 1, jnp.where(upper(col), col - 1, -1))
        return (
            unit,
            (row == mate).astype(f32),
            lower(col),
            lower(row),
            lower(col) | upper(col),
            lower(row) | upper(row),
        )

    return pairing(0), pairing(1)


def eigen_start(cell_col, cell_row, face_col, face_row, low_row, screen_row):
    n = cell_col.shape[0]
    row = lax.broadcasted_iota(jnp.int32, (n, LANES), 0)
    col = lax.broadcasted_iota(jnp.int32, (n, LANES), 1)
    tri = (
        (row == col).astype(f32) * (low_row + face_row + screen_row)
        - (col == row + 1).astype(f32) * face_col
        - (col == row - 1).astype(f32) * face_row
    )
    matrix = tri * (1.0 / jnp.sqrt(cell_col)) * (1.0 / jnp.sqrt(cell_row))
    return jnp.where(col < n, matrix, (col == row + n).astype(f32))


def eigen_finish(held, cell_row, face_row, screen_row):
    n = held.shape[0]
    col = lax.broadcasted_iota(jnp.int32, (n, LANES), 1)
    modes = jnp.where(col < n, pltpu.roll(held, LANES - n, 1), 0.0) / jnp.sqrt(cell_row)
    norm = jnp.sum(cell_row * modes * modes, axis=1, keepdims=True)
    modes = modes * (1.0 / jnp.sqrt(norm))
    slope = pltpu.roll(modes, LANES - 1, 1) - modes
    walls = jnp.where((col == 0) | (col == n - 1), 1.0, 0.0) * face_row[:, n - 1 : n]
    energy = (screen_row + walls) * modes * modes
    energy = energy + jnp.where(col < n - 1, face_row, 0.0) * slope * slope
    return modes, jnp.sum(energy, axis=1, keepdims=True)


def write_tables(modes, fores, backs):
    n = modes.shape[0]
    size = ROWS * n

    def flags(shape, test):
        first = lax.broadcasted_iota(jnp.int32, shape, 0)
        second = lax.broadcasted_iota(jnp.int32, shape, 1)
        return jnp.where(test(first, second), 1.0, 0.0)

    pick_mode = flags((size, n), lambda a, b: a % n == b).astype(bf16)
    spread_mode = flags((n, size), lambda a, b: b % n == a).astype(bf16)
    pick_layer = flags((size, LANES), lambda a, b: a // ROWS == b).astype(bf16)
    spread_layer = flags((LANES, size), lambda a, b: b // ROWS == a).astype(bf16)
    same_fore = flags((size, size), lambda a, b: a // n == b % ROWS)
    same_back = flags((size, size), lambda a, b: a % ROWS == b // n)
    across = (((1,), (1,)), ((), ()))
    for part, fore, back in zip(split(modes), fores, backs):
        turned = jnp.dot(pick_mode, part, preferred_element_type=f32)
        spread = jnp.dot(turned.astype(bf16), spread_layer, preferred_element_type=f32)
        fore[...] = (spread * same_fore).astype(bf16)
        layered = lax.dot_general(pick_layer, part, across, preferred_element_type=f32)
        spread = jnp.dot(layered.astype(bf16), spread_mode, preferred_element_type=f32)
        back[...] = (spread * same_back).astype(bf16)


def raised(base, count):
    value = None
    while count:
        if count & 1:
            value = base if value is None else value * base
        base = base * base
        count >>= 1
    return value


def entering_values(ratio, x_local, blocks, ends):
    across = raised(ratio, x_local)
    around = 1.0 / (1.0 - raised(across, blocks))
    both = ratio * ratio * (1.0 - across * across) / ((1.0 - ratio) * (1.0 + ratio))
    last = ends(blocks - 1, 0)
    for step in reversed(range(blocks - 1)):
        last = ends(step, 0) + across * last
    last = last * around
    tops = []
    enter = last
    for step in reversed(range(blocks)):
        enter = last
        tops.append(ends(step, 1) + both * last)
        last = ends(step, 0) + across * last
    first = tops[-1]
    for top in reversed(tops[:-1]):
        first = top + across * first
    return enter, first * around


def kernel(
    charge_in, fore_high_in, fore_low_in, back_high_in, back_low_in, cell, face, screening, shift,
    out,
    charge, fore_high, fore_low, plain, sent, got, risen, returned, arrived, result, back_high, back_low,
    to_high, to_low, from_high, from_low, ratio_ref, near, far, turn, ends, linked, flow,
    send_sems, recv_sems, return_sems, arrive_sems, link_send, link_recv, table_sems, out_sems,
):
    depth, x_local, width = charge.shape
    slabs = sent.shape[1]
    halves_of, layers, half_part = ratio_ref.shape
    blocks = linked.shape[1]
    part = halves_of * half_part
    rows = x_local // CHUNKS
    tiles = rows // ROWS
    me, place = lax.axis_index("gz"), lax.axis_index("gx")

    tables = [
        pltpu.make_async_copy(back_high_in, back_high, table_sems.at[0]),
        pltpu.make_async_copy(back_low_in, back_low, table_sems.at[1]),
    ]
    early = [
        pltpu.make_async_copy(charge_in, charge, table_sems.at[2]),
        pltpu.make_async_copy(fore_high_in, fore_high, table_sems.at[3]),
        pltpu.make_async_copy(fore_low_in, fore_low, table_sems.at[4]),
    ]
    for table in early + tables:
        table.start()
    barrier = pltpu.get_barrier_semaphore()
    for axis, own, count in (("gz", me, slabs), ("gx", place, blocks)):
        for step in range(1, count):
            other = lax.rem(own + step, count)
            pl.semaphore_signal(barrier, inc=1, device_id={axis: other}, device_id_type=MESH)

    plain[...] = jnp.ones_like(plain)
    for index, value in enumerate((cell, face, screening)):
        plain[index : index + 1, 0:layers] = value[...]
    cell_row, face_row, screen_row = plain[0:1], plain[1:2], plain[2:3]
    unit = lax.broadcasted_iota(jnp.int32, (layers, LANES), 0) == lax.broadcasted_iota(
        jnp.int32, (layers, LANES), 1
    )
    cell_col = jnp.sum(jnp.where(unit, cell_row, 0.0), axis=1, keepdims=True)
    face_col = jnp.sum(jnp.where(unit, face_row, 0.0), axis=1, keepdims=True)
    lane = lax.broadcasted_iota(jnp.int32, (1, LANES), 1)
    low_row = jnp.where(lane == 0, face_row[:, layers - 1 : layers], pltpu.roll(face_row, 1, 1))
    held = eigen_start(cell_col, cell_row, face_col, face_row, low_row, screen_row)
    pairs = pairings(layers)
    turns = -(-(layers.bit_length() - 1) * (layers // 2) // (CHUNKS * slabs))

    def two(_, value):
        return one_stage(one_stage(value, pairs[0]), pairs[1])

    held = lax.fori_loop(0, layers // 2, two, held)
    for table in early:
        table.wait()
    pl.semaphore_wait(barrier, slabs + blocks - 2)

    def send(half, chunk, step):
        slot = half * CHUNKS + chunk
        return pltpu.make_async_remote_copy(
            src_ref=sent.at[slot, step],
            dst_ref=got.at[slot, step],
            send_sem=send_sems.at[slot, step],
            recv_sem=recv_sems.at[slot, step],
            device_id={"gz": lax.rem(me + step, slabs)},
            device_id_type=MESH,
        )

    def forward_y(chunk, held):
        start = pl.multiple_of(chunk * rows, rows)
        left = split(charge[:, pl.ds(start, rows), :].reshape(depth * rows, width))
        for step in list(range(1, slabs)) + [0]:
            other = lax.rem(me + step, slabs)
            value = product(left, (fore_high[other], fore_low[other]))
            for _ in range(turns):
                held = one_stage(one_stage(held, pairs[0]), pairs[1])
            value = value.reshape(depth, rows, part)
            for half in range(halves_of):
                piece = value[:, :, half * half_part : (half + 1) * half_part]
                if step:
                    sent[half * CHUNKS + chunk, step] = piece
                else:
                    got[half * CHUNKS + chunk, 0] = piece
            if step:
                send(0, chunk, step).start()
        return held

    held = lax.fori_loop(0, CHUNKS, forward_y, held)

    def send_rest(chunk, _):
        for half in range(1, halves_of):
            for step in range(1, slabs):
                send(half, chunk, step).start()
        return 0

    lax.fori_loop(0, CHUNKS, send_rest, 0)

    modes, values = eigen_finish(held, cell_row, face_row, screen_row)
    write_tables(modes, (to_high, to_low), (from_high, from_low))
    total = values + shift[me]
    ratio = 2.0 / (2.0 + total + jnp.sqrt(total * (total + 4.0)))
    for half in range(halves_of):
        ratio_ref[half] = ratio[:, half * half_part : (half + 1) * half_part]

    def give_back(half, chunk, step):
        slot = half * CHUNKS + chunk
        other = lax.rem(me + step, slabs)
        return pltpu.make_async_remote_copy(
            src_ref=returned.at[slot, other],
            dst_ref=arrived.at[slot, step],
            send_sem=return_sems.at[slot, step],
            recv_sem=arrive_sems.at[slot, step],
            device_id={"gz": other},
            device_id_type=MESH,
        )

    def solve(half):
        ends[half] = jnp.zeros(ends.shape[1:], f32)
        flow[...] = ratio_ref[half]

        def rise(chunk, _):
            for step in range(1, slabs):
                send(half, chunk, step).wait_recv()

            def tile(index, _):
                start = pl.multiple_of(index * ROWS, ROWS)
                slot = half * CHUNKS + chunk
                parts = [
                    got[slot, lax.rem(me + (slabs - slab), slabs), :, pl.ds(start, ROWS), :]
                    for slab in range(slabs)
                ]
                block = jnp.concatenate(parts, axis=0).reshape(layers * ROWS, half_part)
                turn[...] = product((to_high[...], to_low[...]), split(block))
                ratio = ratio_ref[half]
                value, total, power = ends[half, 0], ends[half, 1], flow[...]
                for x in range(ROWS):
                    value = turn[x * layers : (x + 1) * layers] + ratio * value
                    risen[chunk * rows + start + x] = value
                    total = total + power * value
                    power = power * ratio
                ends[half, 0] = value
                ends[half, 1] = total
                flow[...] = power
                return 0

            lax.fori_loop(0, tiles, tile, 0)
            return 0

        lax.fori_loop(0, CHUNKS, rise, 0)

        links = []
        for step in range(1, blocks):
            copy = pltpu.make_async_remote_copy(
                src_ref=ends.at[half],
                dst_ref=linked.at[half, step],
                send_sem=link_send.at[half, step],
                recv_sem=link_recv.at[half, step],
                device_id={"gx": lax.rem(place + step, blocks)},
                device_id_type=MESH,
            )
            copy.start()
            links.append(copy)
        power = ratio_ref[half]
        for x in range(ROWS):
            near[x] = power
            if x < ROWS - 1:
                power = power * ratio_ref[half]
        for copy in links:
            copy.wait()
        enter, leave = entering_values(
            ratio_ref[half], x_local, blocks,
            lambda step, which: linked[half, step, which] if step else ends[half, which],
        )
        flow[...] = leave
        power = near[ROWS - 1]
        for block in range(x_local // ROWS):
            far[block] = enter
            enter = enter * power

        def fall(turned, _):
            chunk = CHUNKS - 1 - turned

            def tile(turned, _):
                index = tiles - 1 - turned
                start = pl.multiple_of(index * ROWS, ROWS)
                ratio = ratio_ref[half]
                value = flow[...]
                entered = far[chunk * tiles + index]
                for x in reversed(range(ROWS)):
                    value = ratio * (risen[chunk * rows + start + x] + near[x] * entered + value)
                    turn[x * layers : (x + 1) * layers] = value
                flow[...] = value
                solved = product((from_high[...], from_low[...]), split(turn[...]))
                returned[half * CHUNKS + chunk, :, :, pl.ds(start, ROWS), :] = solved.reshape(
                    slabs, depth, ROWS, half_part
                )
                return 0

            lax.fori_loop(0, tiles, tile, 0)
            for step in range(1, slabs):
                give_back(half, chunk, step).start()
            return 0

        lax.fori_loop(0, CHUNKS, fall, 0)

    for half in range(halves_of):
        solve(half)
    for table in tables:
        table.wait()

    def write(chunk):
        place = pl.ds(pl.multiple_of(chunk * rows, rows), rows)
        return pltpu.make_async_copy(
            result.at[chunk], out.at[:, place, :], out_sems.at[chunk]
        )

    def back_y(turned, _):
        chunk = CHUNKS - 1 - turned
        total = None
        for step in range(slabs):
            pieces = []
            for half in range(halves_of):
                slot = half * CHUNKS + chunk
                if step:
                    give_back(half, chunk, step).wait_recv()
                    value = arrived[slot, step]
                else:
                    value = returned[slot, me]
                pieces.append(value.reshape(depth * rows, half_part))
            source = lax.rem(me + (slabs - step), slabs)
            left = split(pieces[0] if halves_of == 1 else jnp.concatenate(pieces, axis=1))
            term = product(left, (back_high[source], back_low[source]))
            total = term if total is None else total + term
        result[chunk] = total.reshape(depth, rows, width)
        write(chunk).start()
        return 0

    lax.fori_loop(0, CHUNKS, back_y, 0)

    def settle(chunk, _):
        for half in range(halves_of):
            for step in range(1, slabs):
                send(half, chunk, step).wait_send()
                give_back(half, chunk, step).wait_send()
        write(chunk).wait()
        return 0

    lax.fori_loop(0, CHUNKS, settle, 0)


def body(charge, cell, face, screening):
    depth, x_local, width = charge.shape
    slabs, blocks = lax.axis_size("gz"), lax.axis_size("gx")
    layers, part, rows = depth * slabs, width // slabs, x_local // CHUNKS
    half_part = HALF if part % HALF == 0 else part
    halves_of = part // half_part
    table = basis_table(width)
    fore = (table * mode_weights(width)[None, :]).reshape(width, slabs, part).transpose(1, 0, 2)
    back = table.T.reshape(slabs, part, width)
    shift = jnp.asarray(mode_shift(width).reshape(slabs, 1, part))
    vmem, anywhere = pl.BlockSpec(memory_space=pltpu.VMEM), pl.BlockSpec(memory_space=pl.ANY)
    slots = halves_of * CHUNKS
    chunked = pltpu.VMEM((slots, slabs, depth, rows, half_part), f32)
    square = pltpu.VMEM((ROWS * layers, ROWS * layers), bf16)
    many = pltpu.SemaphoreType.DMA((slots, slabs))
    return pl.pallas_call(
        kernel,
        out_shape=jax.ShapeDtypeStruct(charge.shape, f32),
        in_specs=[anywhere] * 5 + [vmem] * 4,
        out_specs=anywhere,
        scratch_shapes=[
            pltpu.VMEM(charge.shape, f32),
            pltpu.VMEM((slabs, width, part), bf16),
            pltpu.VMEM((slabs, width, part), bf16),
            pltpu.VMEM((8, LANES), f32),
            chunked,
            chunked,
            pltpu.VMEM((x_local, layers, half_part), f32),
            chunked,
            chunked,
            pltpu.VMEM((CHUNKS, depth, rows, width), f32),
            pltpu.VMEM((slabs, part, width), bf16),
            pltpu.VMEM((slabs, part, width), bf16),
            square,
            square,
            square,
            square,
            pltpu.VMEM((halves_of, layers, half_part), f32),
            pltpu.VMEM((ROWS, layers, half_part), f32),
            pltpu.VMEM((x_local // ROWS, layers, half_part), f32),
            pltpu.VMEM((ROWS * layers, half_part), f32),
            pltpu.VMEM((halves_of, 2, layers, half_part), f32),
            pltpu.VMEM((halves_of, blocks, 2, layers, half_part), f32),
            pltpu.VMEM((layers, half_part), f32),
            many,
            many,
            many,
            many,
            pltpu.SemaphoreType.DMA((halves_of, blocks)),
            pltpu.SemaphoreType.DMA((halves_of, blocks)),
            pltpu.SemaphoreType.DMA((5,)),
            pltpu.SemaphoreType.DMA((CHUNKS,)),
        ],
        compiler_params=pltpu.CompilerParams(
            collective_id=0, has_side_effects=True, vmem_limit_bytes=VMEM
        ),
        cost_estimate=pl.CostEstimate(
            flops=12 * depth * x_local * width * width,
            bytes_accessed=8 * charge.size,
            transcendentals=0,
        ),
        name="precondition",
    )(
        charge, *halves(fore), *halves(back), cell[None], face[None], screening[None], shift
    )


def solution(mesh):
    in_specs = (P("gz", "gx", None), P(), P(), P())
    out_specs = P("gz", "gx", None)
    return jax.shard_map(body, mesh=mesh, in_specs=in_specs, out_specs=out_specs, check_vma=False)
```
